32 devices in a mesh: tm: 8 (over z, x), height: 4 (over y, core).
Axes of the slice: x: 2, y: 2, z: 4, core: 2. Of those that a mesh axis runs over, the one named last changes fastest.
Arguments:
- frames_in: bfloat16 [512, 128, 1024], P('tm', 'height'), may hold values from -6 to 6
- time_filter: bfloat16 [512, 64], replicated, may hold values from -0.25 to 0.25
- height_filter: bfloat16 [128, 64], replicated, may hold values from -0.5 to 0.5
Outputs:
- layer_out: bfloat16 [512, 128, 1024], P('tm', 'height')
The draws below stay inside these ranges and needn't reach their ends.
All inputs are finite; a program needn't handle non-finite values.
Results may differ from the reference program's by a relative error of at most 0.0051.
Values may be sent and summed in bfloat16 or wider, within the bound.
No kernel may reach another device: no remote copies, remote signals or barrier semaphores. Data moves between devices by JAX's collectives and lax.ppermute only.
A program may use at most 128 MiB of HBM per device.

```python
import jax
import jax.numpy as jnp

FRAMES = 512
HEIGHT = 128
CH = 64
LANES = 1024


def block_scale(key, dims, pieces, low, high):
    gain, own = 1.0, jax.random.fold_in(key, 6)
    for axis_at, blocks in pieces:
        steps = jnp.exp(jax.random.uniform(jax.random.fold_in(own, axis_at), (blocks,), jnp.float32, low / len(pieces), high / len(pieces)))
        gain = gain * jnp.repeat(steps, dims[axis_at] // blocks).reshape([-1 if axis == axis_at else 1 for axis in range(len(dims))])
    return gain


def scatter_about(own_key, shape, width, reach, cuts=(), dtype=jnp.bfloat16):
    level = block_scale(own_key, shape, cuts, -0.22, 0.18) if cuts else 1.0
    values = jax.random.normal(own_key, shape, jnp.float32) * width * level
    return jnp.minimum(jnp.maximum(values, -reach), reach).astype(dtype)


def setup_inputs(seed: int = 0) -> dict:
    splits = jax.random.split(jax.random.key(seed), 4)
    frames_in = scatter_about(splits[0], (FRAMES, HEIGHT, LANES), 1.0, 6.0, ((0, 8), (1, 4)))
    time_filter = scatter_about(splits[1], (FRAMES, CH), FRAMES ** -0.5, 0.25)
    height_filter = scatter_about(splits[2], (HEIGHT, CH), HEIGHT ** -0.5, 0.5)
    return dict(frames_in=frames_in, time_filter=time_filter, height_filter=height_filter)


def reference(frames_in, time_filter, height_filter):
    lane_total = frames_in.shape[2]
    across = lane_total // CH
    signal = frames_in.astype(jnp.float32).reshape(FRAMES, HEIGHT, across, CH)
    spectrum = jnp.fft.rfft(signal, axis=0)
    kernel = jnp.fft.rfft(time_filter.astype(jnp.float32), axis=0)[:, None, None, :]
    temporal = jnp.fft.irfft(spectrum * kernel, n=FRAMES, axis=0).astype(jnp.bfloat16)
    row_spectrum = jnp.fft.rfft(temporal.astype(jnp.float32), axis=1)
    row_kernel = jnp.fft.rfft(height_filter.astype(jnp.float32), axis=0)[None, :, None, :]
    spatial = jnp.fft.irfft(row_spectrum * row_kernel, n=HEIGHT, axis=1).astype(jnp.bfloat16)
    spatial = spatial.reshape(FRAMES, HEIGHT, lane_total)
    return (frames_in.astype(jnp.float32) + spatial.astype(jnp.float32)).astype(jnp.bfloat16)
```

```python
import functools

import jax
import jax.numpy as jnp
import numpy as np
from jax import lax
from jax.experimental import pallas as pl
from jax.experimental.pallas import tpu as pltpu
from jax.sharding import PartitionSpec as P

F32, BF16 = jnp.float32, jnp.bfloat16
TILE = 128
VMEM_BYTES = 24 << 20


def split_terms(table):
    high = table.astype(jnp.bfloat16)
    low = (table - high.astype(np.float64)).astype(jnp.bfloat16)
    return high, low


def fourier_tables(size):
    half = size // 2
    wave, at = np.arange(half)[:, None], np.arange(size)[None, :]
    angle = 2.0 * np.pi * ((wave * at) % size) / size
    sines = np.sin(angle)
    sines[0] = 1.0 - 2.0 * (np.arange(size) % 2)
    analysis = np.concatenate([np.cos(angle), sines], axis=0)
    weight = np.full((size,), 2.0 / size)
    weight[0] = weight[half] = 1.0 / size
    synthesis = (analysis * weight[:, None]).T
    return split_terms(analysis) + split_terms(synthesis)


def filter_spectrum(taps, tables):
    size, channels = taps.shape
    half = size // 2
    sums = jnp.dot(tables[0], taps, preferred_element_type=F32) + jnp.dot(tables[1], taps, preferred_element_type=F32)
    cosines, sines = sums[:half], sums[half:]
    first = lax.broadcasted_iota(jnp.int32, (half, channels), 0) == 0
    spectrum = jnp.stack([cosines, jnp.where(first, 0.0, sines), jnp.where(first, sines, cosines)])
    return jnp.tile(spectrum, (1, 1, TILE // channels))


def filtered(signal, spectrum, tables):
    half = spectrum.shape[1]
    analysis_high, analysis_low, synthesis_high, synthesis_low = (t[...] for t in tables)
    coef = jnp.dot(analysis_high, signal, preferred_element_type=F32)
    coef += jnp.dot(analysis_low, signal, preferred_element_type=F32)
    cos_part, sin_part = coef[:half], coef[half:]
    keep, turn, other = (jnp.concatenate([spectrum[n]] * (signal.shape[1] // TILE), axis=1) for n in range(3))
    product = jnp.concatenate([cos_part * keep - sin_part * turn, sin_part * other + cos_part * turn], axis=0)
    high = product.astype(BF16)
    low = (product - high.astype(F32)).astype(BF16)
    result = jnp.dot(synthesis_high, high, preferred_element_type=F32)
    result += jnp.dot(synthesis_low, high, preferred_element_type=F32)
    result += jnp.dot(synthesis_high, low, preferred_element_type=F32)
    return result


def sends_to(me, slot, count):
    return me ^ slot if count & (count - 1) == 0 else (me + slot) % count


def comes_from(me, slot, count):
    return me ^ slot if count & (count - 1) == 0 else (me + count - slot) % count


def exchange(pieces, axis):
    count = len(pieces)
    return [pieces[0]] + [
        lax.ppermute(piece, axis, [(n, sends_to(n, slot, count)) for n in range(count)])
        for slot, piece in enumerate(pieces)
        if slot
    ]


def call(kernel, operands, out_shapes, scratch=(), flops=0, aliases={}):
    return pl.pallas_call(
        kernel,
        in_specs=[pl.BlockSpec(memory_space=pltpu.VMEM)] * len(operands),
        out_specs=[pl.BlockSpec(memory_space=pltpu.VMEM)] * len(out_shapes),
        out_shape=[jax.ShapeDtypeStruct(s, BF16) for s in out_shapes],
        scratch_shapes=list(scratch),
        input_output_aliases=aliases,
        compiler_params=pltpu.CompilerParams(vmem_limit_bytes=VMEM_BYTES),
        cost_estimate=pl.CostEstimate(
            flops=flops, bytes_accessed=4 * sum(int(np.prod(s)) for s in out_shapes), transcendentals=0
        ),
    )(*operands)


class Layout:
    def __init__(self, frames, rows, width, tm, height):
        self.frames, self.rows, self.width, self.tm, self.height = frames, rows, width, tm, height
        self.tiles = width // TILE
        self.own_rows = rows // (tm // self.tiles)

    def place(self, device):
        return device // self.tiles * self.own_rows, device % self.tiles


def pack_kernel(cut, *refs):
    inputs, outputs, (wide,) = refs[: -1 - cut.tm], refs[-1 - cut.tm : -1], refs[-1:]
    me, mine = lax.axis_index("tm"), lax.axis_index("height")
    run = cut.frames // len(inputs)
    for slot, ref in enumerate(inputs):
        start = comes_from(mine, slot, len(inputs)) * run * cut.rows if len(inputs) > 1 else 0
        for tile in range(cut.tiles):
            block = ref[:, :, tile * TILE : (tile + 1) * TILE].astype(F32).reshape(run * cut.rows, TILE)
            wide[tile, pl.ds(pl.multiple_of(start, 8), run * cut.rows), :] = block
    for slot, ref in enumerate(outputs):
        row, tile = cut.place(sends_to(me, slot, cut.tm))
        for r in range(cut.own_rows):
            ref[r] = wide[tile, pl.ds(row + r, cut.frames, stride=cut.rows), :].astype(BF16)


def unpack(cut, inputs, wide):
    me = lax.axis_index("tm")
    for slot, ref in enumerate(inputs):
        row, tile = cut.place(comes_from(me, slot, cut.tm))
        for r in range(cut.own_rows):
            wide[tile, pl.ds(row + r, cut.frames, stride=cut.rows), :] = ref[r].astype(F32)


def unpack_kernel(cut, *refs):
    inputs, outputs, wide = refs[: cut.tm], refs[cut.tm : -1], refs[-1]
    unpack(cut, inputs, wide)
    mine = lax.axis_index("height")
    run = cut.frames // cut.height
    for slot, ref in enumerate(outputs):
        start = sends_to(mine, slot, cut.height) * run * cut.rows
        for tile in range(cut.tiles):
            block = wide[tile, pl.ds(pl.multiple_of(start, 8), run * cut.rows), :]
            ref[:, :, tile * TILE : (tile + 1) * TILE] = block.reshape(run, cut.rows, TILE).astype(BF16)


def unpack_add_kernel(cut, *refs):
    inputs, (x_ref, _, out_ref, wide) = refs[: cut.tm], refs[cut.tm :]
    unpack(cut, inputs, wide)
    for tile in range(cut.tiles):
        lanes = slice(tile * TILE, (tile + 1) * TILE)
        added = wide[tile].reshape(cut.frames, cut.rows, TILE)
        out_ref[:, :, lanes] = (x_ref[:, :, lanes].astype(F32) + added).astype(BF16)


def time_kernel(cut, *refs):
    inputs, spectrum, tables = refs[: cut.tm], refs[cut.tm], refs[cut.tm + 1 : cut.tm + 5]
    outputs, signal, result = refs[cut.tm + 5 : -2], refs[-2], refs[-1]
    me = lax.axis_index("tm")
    for slot, ref in enumerate(inputs):
        at = pl.ds(pl.multiple_of(comes_from(me, slot, cut.tm) * cut.frames, 16), cut.frames)
        for r in range(cut.own_rows):
            signal[at, r * TILE : (r + 1) * TILE] = ref[r]
    step = min(2, cut.own_rows)
    for first in range(0, cut.own_rows, step):
        lanes = slice(first * TILE, (first + step) * TILE)
        result[:, lanes] = filtered(signal[:, lanes], spectrum[...], tables).astype(BF16)
    for slot, ref in enumerate(outputs):
        at = pl.ds(pl.multiple_of(sends_to(me, slot, cut.tm) * cut.frames, 16), cut.frames)
        for r in range(cut.own_rows):
            ref[r] = result[at, r * TILE : (r + 1) * TILE]


def rows_kernel(cut, *refs):
    inputs, spectrum, tables = refs[: cut.height], refs[cut.height], refs[cut.height + 1 : cut.height + 5]
    outputs, signal, result = refs[cut.height + 5 : -2], refs[-2], refs[-1]
    mine = lax.axis_index("height")
    run = cut.frames // cut.height
    for f in range(run):
        for slot, ref in enumerate(inputs):
            at = pl.ds(pl.multiple_of(comes_from(mine, slot, cut.height) * cut.rows, 8), cut.rows)
            signal[at, :] = ref[f].astype(F32)
        result[...] = filtered(signal[...].astype(BF16), spectrum[...], tables)
        for slot, ref in enumerate(outputs):
            at = pl.ds(pl.multiple_of(sends_to(mine, slot, cut.height) * cut.rows, 8), cut.rows)
            ref[f] = result[at, :].astype(BF16)


def add_kernel(cut, *refs):
    inputs, (x_ref, _, out_ref) = refs[: cut.height], refs[cut.height :]
    mine = lax.axis_index("height")
    run = cut.frames // cut.height
    for slot, ref in enumerate(inputs):
        at = pl.ds(comes_from(mine, slot, cut.height) * run, run)
        out_ref[at] = (x_ref[at].astype(F32) + ref[...].astype(F32)).astype(BF16)


def add_part(kernel, cut, pieces, frames_in, so_far, part, scratch=()):
    block = pl.BlockSpec((cut.frames, cut.rows, cut.width), lambda n: (0, 0, part))
    whole = [pl.BlockSpec(p.shape, lambda n: (0, 0, 0)) for p in pieces]
    held = frames_in if so_far is None else so_far
    return pl.pallas_call(
        functools.partial(kernel, cut),
        grid=(1,),
        in_specs=whole + [block, pl.BlockSpec(memory_space=pl.ANY)],
        out_specs=block,
        out_shape=jax.ShapeDtypeStruct(frames_in.shape, BF16),
        scratch_shapes=list(scratch),
        input_output_aliases={} if so_far is None else {len(pieces) + 1: 0},
        compiler_params=pltpu.CompilerParams(vmem_limit_bytes=VMEM_BYTES),
        cost_estimate=pl.CostEstimate(
            flops=0, bytes_accessed=6 * cut.frames * cut.rows * cut.width, transcendentals=0
        ),
    )(*pieces, frames_in, held)


def plan(tm, rows, lanes):
    for parts in (4, 2, 1):
        tiles = lanes // parts // TILE
        if tiles and lanes % (parts * TILE) == 0 and tm % tiles == 0 and rows % (tm // tiles) == 0:
            return parts
    raise ValueError("no plan")


def shards(frames_in, time_taps, row_taps):
    frames, rows, lanes = frames_in.shape
    tm, height = lax.axis_size("tm"), lax.axis_size("height")
    parts = plan(tm, rows, lanes)
    width = lanes // parts
    cut = Layout(frames, rows, width, tm, height)
    run = frames // height
    time_tables, row_tables = fourier_tables(frames * tm), fourier_tables(rows * height)
    time_spectrum = filter_spectrum(time_taps, time_tables)
    row_spectrum = filter_spectrum(row_taps, row_tables)
    time_piece, row_piece = (cut.own_rows, frames, TILE), (run, rows, width)
    wide = pltpu.VMEM((cut.tiles, frames * rows, TILE), F32)

    def pack(pieces):
        return call(functools.partial(pack_kernel, cut), pieces, [time_piece] * tm, [wide])

    def along_time(pieces):
        pieces = exchange(pieces, "tm")
        size = frames * tm
        buffer = pltpu.VMEM((size, cut.own_rows * TILE), BF16)
        operands = list(pieces) + [time_spectrum, *time_tables]
        flops = 10 * size * size * cut.own_rows * TILE
        pieces = call(functools.partial(time_kernel, cut), operands, [time_piece] * tm, [buffer, buffer], flops)
        return exchange(pieces, "tm")

    def along_rows(pieces):
        pieces = exchange(pieces, "height")
        size = rows * height
        buffer = pltpu.VMEM((size, width), F32)
        operands = list(pieces) + [row_spectrum, *row_tables]
        flops = 10 * size * size * run * width
        pieces = call(functools.partial(rows_kernel, cut), operands, [row_piece] * height, [buffer, buffer], flops)
        return exchange(pieces, "height")

    mine = lax.axis_index("height")
    so_far = None
    for part in range(parts):
        if part < parts // 2:
            x = lax.slice_in_dim(frames_in, part * width, (part + 1) * width, axis=2)
            pieces = along_time(pack([x]))
            pieces = call(functools.partial(unpack_kernel, cut), pieces, [row_piece] * height, [wide])
            pieces = along_rows(pieces)
            so_far = add_part(add_kernel, cut, pieces, frames_in, so_far, part)
        else:
            pieces = [
                lax.dynamic_slice(frames_in, (sends_to(mine, slot, height) * run, 0, part * width), row_piece)
                for slot in range(height)
            ]
            pieces = along_time(pack(along_rows(pieces)))
            so_far = add_part(unpack_add_kernel, cut, pieces, frames_in, so_far, part, [wide])
    return so_far


def solution(mesh):
    return jax.shard_map(
        shards,
        mesh=mesh,
        in_specs=(P("tm", "height", None), P(), P()),
        out_specs=P("tm", "height", None),
        check_vma=False,
    )
```

```python
import functools

import jax
import jax.numpy as jnp
import numpy as np
from jax import lax
from jax.experimental import pallas as pl
from jax.experimental.pallas import tpu as pltpu
from jax.sharding import PartitionSpec as P

F32, BF16 = jnp.float32, jnp.bfloat16
TILE = 128
WIDE = 2 * TILE
PARTS = 2
VMEM_BYTES = 60 << 20
STEPS = 4
ANYWHERE = pl.BlockSpec(memory_space=pl.ANY)


def split_terms(table):
    high = table.astype(jnp.bfloat16)
    low = (table - high.astype(np.float64)).astype(jnp.bfloat16)
    return high, low


def fourier_tables(size):
    half = size // 2
    wave, at = np.arange(half)[:, None], np.arange(size)[None, :]
    angle = 2.0 * np.pi * ((wave * at) % size) / size
    sines = np.sin(angle)
    sines[0] = 1.0 - 2.0 * (np.arange(size) % 2)
    analysis = np.concatenate([np.cos(angle), sines], axis=0)
    weight = np.full((size,), 2.0 / size)
    weight[0] = weight[half] = 1.0 / size
    synthesis = (analysis * weight[:, None]).T
    return split_terms(analysis) + split_terms(synthesis)


def spectrum_kernel(taps_ref, high_ref, low_ref, out_ref):
    half = taps_ref.shape[0] // 2
    sums = jnp.dot(high_ref[...], taps_ref[...], preferred_element_type=F32)
    sums += jnp.dot(low_ref[...], taps_ref[...], preferred_element_type=F32)
    cosines, sines = sums[:half], sums[half:]
    first = lax.broadcasted_iota(jnp.int32, cosines.shape, 0) == 0
    out_ref[0] = cosines
    out_ref[1] = jnp.where(first, 0.0, sines)
    out_ref[2] = jnp.where(first, sines, cosines)


def filtered(signal, spectrum, tables):
    half = spectrum.shape[1]
    analysis_high, analysis_low, synthesis_high, synthesis_low = (t[...] for t in tables)
    coef = jnp.dot(analysis_high, signal, preferred_element_type=F32)
    coef += jnp.dot(analysis_low, signal, preferred_element_type=F32)
    cos_part, sin_part = coef[:half], coef[half:]
    keep, turn, other = (jnp.concatenate([spectrum[n]] * (signal.shape[1] // TILE), axis=1) for n in range(3))
    product = jnp.concatenate([cos_part * keep - sin_part * turn, sin_part * other + cos_part * turn], axis=0)
    high = product.astype(BF16)
    low = (product - high.astype(F32)).astype(BF16)
    result = jnp.dot(synthesis_high, high, preferred_element_type=F32)
    result += jnp.dot(synthesis_low, high, preferred_element_type=F32)
    result += jnp.dot(synthesis_high, low, preferred_element_type=F32)
    return result


class Cut:
    def __init__(self, frames, rows, width, tm, height):
        self.frames, self.rows, self.width, self.tm, self.height = frames, rows, width, tm, height
        self.devices = tm * height
        self.own = width // self.devices
        self.block = TILE // self.own
        self.blocks = rows // self.block
        self.tiles = width // TILE
        self.piece = (self.blocks, frames, TILE)

    @staticmethod
    def fits(frames, rows, lanes, tm, height):
        own = lanes // PARTS // (tm * height)
        if own == 0 or TILE % own or lanes != PARTS * own * tm * height:
            return False
        block = TILE // own
        return rows % block == 0 and (lanes // PARTS) % TILE == 0 and rows * height * own % WIDE == 0 and frames % 16 == 0


def call(kernel, ins, outs, scratch=(), flops=0, held=None, dtype=BF16):
    unread = [] if held is None else [held]

    def body(*refs):
        kernel(*refs[: len(ins)], *refs[len(ins) + len(unread) :])

    moved = 2 * sum(int(np.prod(a.shape)) for a, _ in ins) + 2 * sum(int(np.prod(s)) for s, _ in outs)
    return pl.pallas_call(
        body,
        grid=(1,),
        in_specs=[spec for _, spec in ins] + [ANYWHERE] * len(unread),
        out_specs=[spec for _, spec in outs],
        out_shape=[jax.ShapeDtypeStruct(shape, dtype) for shape, _ in outs],
        scratch_shapes=list(scratch),
        input_output_aliases={} if held is None else {len(ins): 0},
        compiler_params=pltpu.CompilerParams(vmem_limit_bytes=VMEM_BYTES),
        cost_estimate=pl.CostEstimate(flops=flops, bytes_accessed=moved, transcendentals=0),
    )(*[array for array, _ in ins], *unread)


def whole(table):
    return table, pl.BlockSpec(table.shape, lambda n: (0,) * table.ndim)


def start_all(copies):
    for copy in copies:
        copy.start()
    return copies


def wait_all(copies):
    for copy in copies:
        copy.wait()


def load(pairs, sems, first=0):
    return start_all([pltpu.make_async_copy(a, b, sems.at[first + n]) for n, (a, b) in enumerate(pairs)])


def frame_runs(cut):
    step = cut.frames // steps_of(cut.frames, 16)
    return [pl.ds(first, step) for first in range(0, cut.frames, step)]


def shuffle_table(cut):
    count = cut.block * TILE
    row, device, lane = np.meshgrid(np.arange(cut.block), np.arange(cut.block), np.arange(cut.own), indexing="ij")
    table = np.zeros((count, count), np.float32)
    table[row * TILE + device * cut.own + lane, device * TILE + row * cut.own + lane] = 1
    return table.astype(jnp.bfloat16)


def pack_kernel(lane, cut, x_ref, shuffle_ref, out_ref, x_buf, shuffle, wide, out_buf, sems):
    tiles = [pl.ds(lane + tile * TILE, TILE) for tile in range(cut.tiles)]
    arriving = load([(x_ref.at[:, :, at], x_buf.at[tile]) for tile, at in enumerate(tiles)], sems)
    (table,) = load([(shuffle_ref, shuffle)], sems, 2 * cut.tiles)
    leaving = []
    for tile in range(cut.tiles):
        arriving[tile].wait()
        wide[...] = x_buf[tile].astype(F32).reshape(cut.frames * cut.rows, TILE)
        rows = [
            jnp.concatenate(
                [
                    wide[pl.ds(block * cut.block + row, cut.frames, stride=cut.rows), :].astype(BF16)
                    for row in range(cut.block)
                ],
                axis=1,
            )
            for block in range(cut.blocks)
        ]
        if tile == 0:
            table.wait()
        moved = jnp.dot(jnp.concatenate(rows, axis=0), shuffle[...], preferred_element_type=F32).astype(BF16)
        first = tile * cut.block
        for n in range(cut.block):
            piece = moved[:, n * TILE : (n + 1) * TILE]
            out_buf[first + n] = piece.reshape(cut.blocks, cut.frames, TILE)
        part = pl.ds(first, cut.block)
        leaving += load([(out_buf.at[part], out_ref.at[part])], sems, cut.tiles + tile)
    wait_all(leaving)


def unpack_add_kernel(lane, cut, y_ref, x_ref, shuffle_ref, out_ref, y_buf, x_buf, shuffle, wide, sems):
    tiles = [pl.ds(lane + tile * TILE, TILE) for tile in range(cut.tiles)]
    parts = [pl.ds(tile * cut.block, cut.block) for tile in range(cut.tiles)]
    (table,) = load([(shuffle_ref, shuffle)], sems, 3 * cut.tiles)
    arriving = load([(y_ref.at[part], y_buf.at[part]) for part in parts], sems)
    added = load([(x_ref.at[:, :, at], x_buf.at[tile]) for tile, at in enumerate(tiles)], sems, cut.tiles)
    table.wait()
    leaving = []
    for tile in range(cut.tiles):
        arriving[tile].wait()
        pieces = [y_buf[tile * cut.block + n].reshape(cut.blocks * cut.frames, TILE) for n in range(cut.block)]
        moved = lax.dot_general(
            jnp.concatenate(pieces, axis=1), shuffle[...], (((1,), (1,)), ((), ())), preferred_element_type=F32
        )
        for block in range(cut.blocks):
            for row in range(cut.block):
                rows = moved[block * cut.frames : (block + 1) * cut.frames, row * TILE : (row + 1) * TILE]
                wide[pl.ds(block * cut.block + row, cut.frames, stride=cut.rows), :] = rows
        added[tile].wait()
        total = x_buf[tile].astype(F32) + wide[...].reshape(cut.frames, cut.rows, TILE)
        x_buf[tile] = total.astype(BF16)
        leaving += load([(x_buf.at[tile], out_ref.at[:, :, tiles[tile]])], sems, 2 * cut.tiles + tile)
    wait_all(leaving)


def filter_kernel(cut, x_ref, spectrum_ref, analysis_h, analysis_l, synthesis_h, synthesis_l, rows_ref, out_ref, *bufs):
    x_buf, temporal, spectrum, *tables, row_table, sems = bufs
    every = cut.height * cut.blocks
    count = len(tables)
    arriving = load([(x_ref, x_buf), (spectrum_ref, spectrum)], sems)
    arriving += load(zip((analysis_h, analysis_l, synthesis_h, synthesis_l), tables), sems, 2)
    (rows_table,) = load([(rows_ref, row_table)], sems, 2 + count)
    wait_all(arriving)

    def column(n):
        source, block = n // cut.blocks, n % cut.blocks
        return jnp.concatenate([x_buf[i * cut.height + source, block] for i in range(cut.tm)], axis=0)

    for n in range(0, every, 2):
        signal = jnp.concatenate([column(n), column(n + 1)], axis=1)
        temporal[:, n * TILE : (n + 2) * TILE] = filtered(signal, spectrum[...], tables).astype(BF16)
    rows_table.wait()
    pairs = every // 2
    for n in range(pairs):
        matrix = row_table[(pairs - 1 - n) * WIDE : (2 * pairs - 1 - n) * WIDE, :]
        result = jnp.dot(temporal[...], matrix, preferred_element_type=F32).astype(BF16)
        for half in range(2):
            source, block = (2 * n + half) // cut.blocks, (2 * n + half) % cut.blocks
            for i in range(cut.tm):
                at = slice(i * cut.frames, (i + 1) * cut.frames)
                x_buf[i * cut.height + source, block] = result[at, half * TILE : (half + 1) * TILE]
    wait_all(load([(x_buf, out_ref)], sems))


def row_matrices(cut, taps):
    size, own = taps.shape
    near = WIDE // own
    pairs = size // near
    far = np.arange(2 * pairs - 1)[:, None, None]
    source, target = np.arange(near)[None, :, None], np.arange(near)[None, None, :]
    index = ((2 * pairs - 1 - far - pairs) * near + target - source) % size
    chosen = (index.reshape(-1, 1) == np.arange(size)[None, :]).astype(jnp.bfloat16)
    picked = jnp.dot(chosen, taps, preferred_element_type=F32).astype(BF16)
    picked = picked.reshape((2 * pairs - 1) * near, 1, WIDE)
    same = jnp.asarray(np.tile(np.eye(own), (1, near)).astype(jnp.bfloat16))
    return (picked * same[None]).reshape((2 * pairs - 1) * WIDE, WIDE)


def shards(frames_in, time_taps, row_taps):
    frames, rows, lanes = frames_in.shape
    tm, height = lax.axis_size("tm"), lax.axis_size("height")
    if not Cut.fits(frames, rows, lanes, tm, height):
        return narrow_shards(frames_in, time_taps, row_taps)
    width = lanes // PARTS
    cut = Cut(frames, rows, width, tm, height)
    size = frames * tm
    tables, shuffle = fourier_tables(size), jnp.asarray(shuffle_table(cut))
    device = lax.axis_index("tm") * height + lax.axis_index("height")

    def free(*arrays):
        return [(array, ANYWHERE) for array in arrays]

    shape = (cut.devices,) + cut.piece
    sems = pltpu.SemaphoreType.DMA((3 * cut.tiles + 8,))
    tile_buf, table_buf = pltpu.VMEM((cut.tiles, frames, rows, TILE), BF16), pltpu.VMEM(shuffle.shape, BF16)
    wide, piece_buf = pltpu.VMEM((frames * rows, TILE), F32), pltpu.VMEM(shape, BF16)

    def exchange(pieces):
        flat = pieces.reshape(cut.devices, cut.blocks * frames, TILE)
        return lax.all_to_all(flat, ("tm", "height"), 0, 0, tiled=True).reshape(shape)

    def pack(part):
        kernel = functools.partial(pack_kernel, part * width, cut)
        scratch = [tile_buf, table_buf, wide, piece_buf, sems]
        return exchange(call(kernel, free(frames_in, shuffle), free(shape), scratch)[0])

    def own_lanes(taps, part):
        first = (part * width + device * cut.own) % taps.shape[1]
        return lax.dynamic_slice_in_dim(taps, first, cut.own, axis=1)

    def both(pieces, part):
        taps = jnp.tile(own_lanes(time_taps, part), (1, TILE // cut.own))
        out = ((3, size // 2, TILE), pl.BlockSpec((3, size // 2, TILE), lambda n: (0, 0, 0)))
        (spectrum,) = call(spectrum_kernel, [whole(t) for t in (taps, *tables[:2])], [out], dtype=F32)
        matrices = row_matrices(cut, own_lanes(row_taps, part))
        every = rows * height * cut.own
        scratch = [piece_buf, pltpu.VMEM((size, every), BF16), pltpu.VMEM(spectrum.shape, F32)]
        scratch += [pltpu.VMEM(t.shape, BF16) for t in (*tables, matrices)] + [sems]
        ins = free(pieces, spectrum, *tables, matrices)
        flops = 2 * size * every * (5 * size + every)
        return exchange(call(functools.partial(filter_kernel, cut), ins, free(shape), scratch, flops)[0])

    def unpack_add(pieces, part, held):
        kernel = functools.partial(unpack_add_kernel, part * width, cut)
        scratch = [piece_buf, tile_buf, table_buf, wide, sems]
        return call(kernel, free(pieces, frames_in, shuffle), free(frames_in.shape), scratch, held=held)[0]

    arrived = [pack(part) for part in range(PARTS)]
    returned = [both(pieces, part) for part, pieces in enumerate(arrived)]
    out = None
    for part, pieces in enumerate(returned):
        out = unpack_add(pieces, part, out)
    return out


def lane_taps(tap_table, first_lane, lane_count):
    channels = tap_table.shape[1]
    distinct = min(lane_count, channels)
    lane_ids = (first_lane + lax.iota(jnp.int32, distinct)) % channels
    selector = (lane_ids[None, :] == lax.iota(jnp.int32, channels)[:, None]).astype(tap_table.dtype)
    picked = jnp.dot(tap_table, selector, preferred_element_type=jnp.float32).astype(
        tap_table.dtype
    )
    return jnp.transpose(picked)


def shifted_taps(taps, base, size):
    distinct, period = taps.shape
    start = (base - (size - 1)) % period
    tiled = jnp.concatenate([taps, taps, taps], axis=1)
    window = lax.slice_in_dim(tiled, start, start + 2 * size - 1, axis=1)
    reversed_window = window[:, ::-1]
    padded = jnp.concatenate([reversed_window, jnp.zeros((distinct, 1), taps.dtype)], axis=1)
    repeated = jnp.tile(padded, (1, size + 1))
    flat = lax.slice_in_dim(repeated, size - 1, size - 1 + size * (2 * size - 1), axis=1)
    return flat.reshape(distinct, size, 2 * size - 1)[:, :, :size]


def time_convolve(segment, own_taps):
    frames, rows_here, lane_count = segment.shape
    distinct = own_taps.shape[0]
    columns = lane_count // distinct
    block_len = min(128, frames)
    block_count = frames // block_len
    blocked = segment.reshape(block_count, block_len, rows_here, columns, distinct)
    blocked = jnp.transpose(blocked, (4, 3, 2, 0, 1))
    running = jnp.zeros((distinct, columns, rows_here, block_count, block_len), jnp.float32)
    for lag_index in range(block_count):
        toeplitz = shifted_taps(own_taps, lag_index * block_len, block_len)
        rolled = jnp.roll(blocked, lag_index, axis=3)
        running = running + jnp.einsum(
            "cab,cxrnb->cxrna", toeplitz, rolled, preferred_element_type=jnp.float32
        )
    result = jnp.transpose(running, (3, 4, 2, 1, 0)).reshape(frames, rows_here, lane_count)
    return result.astype(jnp.bfloat16)


def row_convolve(segment, row_taps):
    frames, height, lane_count = segment.shape
    distinct = row_taps.shape[0]
    columns = lane_count // distinct
    arranged = jnp.transpose(segment.reshape(frames, height, columns, distinct), (3, 2, 0, 1))
    circulant = shifted_taps(row_taps, 0, height)
    filtered = jnp.einsum("cab,cxfb->cxfa", circulant, arranged, preferred_element_type=jnp.float32)
    result = jnp.transpose(filtered, (2, 3, 1, 0)).reshape(frames, height, lane_count)
    return result.astype(jnp.bfloat16)


def narrow_shards(frames_in, time_filter, height_filter):
    frames_dev, rows_dev, lane_total = frames_in.shape
    tm_count = lax.axis_size("tm")
    height_count = lax.axis_size("height")
    lane_count = lane_total // (tm_count * height_count)
    first_lane = (
        lax.axis_index("tm") * (lane_total // tm_count) + lax.axis_index("height") * lane_count
    )
    own_taps = lane_taps(time_filter, first_lane, lane_count)
    row_taps = lane_taps(height_filter, first_lane, lane_count)
    gathered = lax.all_to_all(
        lax.all_to_all(frames_in, "tm", split_axis=2, concat_axis=0, tiled=True),
        "height",
        split_axis=2,
        concat_axis=1,
        tiled=True,
    )
    temporal = time_convolve(gathered, own_taps)
    spatial_lanes = row_convolve(temporal, row_taps)
    returned = lax.all_to_all(
        lax.all_to_all(spatial_lanes, "tm", split_axis=0, concat_axis=2, tiled=True),
        "height",
        split_axis=1,
        concat_axis=2,
        tiled=True,
    )
    spatial = returned.reshape(frames_dev, rows_dev, height_count, tm_count, lane_count)
    spatial = jnp.transpose(spatial, (0, 1, 3, 2, 4)).reshape(frames_dev, rows_dev, lane_total)
    return (frames_in.astype(jnp.float32) + spatial.astype(jnp.float32)).astype(jnp.bfloat16)


def solution(mesh):
    return jax.shard_map(
        shards,
        mesh=mesh,
        in_specs=(P("tm", "height", None), P(), P()),
        out_specs=P("tm", "height", None),
        check_vma=False,
    )
```

```python
import functools

import jax
import jax.numpy as jnp
import numpy as np
from jax import lax
from jax.experimental import pallas as pl
from jax.experimental.pallas import tpu as pltpu
from jax.sharding import PartitionSpec as P

F32, BF16 = jnp.float32, jnp.bfloat16
TILE = 128
WIDE = 2 * TILE
PARTS = 2
VMEM_BYTES = 62 << 20
FILTER_VMEM = 40 << 20
STEPS = 4
ANYWHERE = pl.BlockSpec(memory_space=pl.ANY)


def split_terms(table):
    high = table.astype(jnp.bfloat16)
    low = (table - high.astype(np.float64)).astype(jnp.bfloat16)
    return high, low


def fourier_tables(size):
    half = size // 2
    wave, at = np.arange(half)[:, None], np.arange(size)[None, :]
    angle = 2.0 * np.pi * ((wave * at) % size) / size
    sines = np.sin(angle)
    sines[0] = 1.0 - 2.0 * (np.arange(size) % 2)
    analysis = np.concatenate([np.cos(angle), sines], axis=0)
    weight = np.full((size,), 2.0 / size)
    weight[0] = weight[half] = 1.0 / size
    synthesis = (analysis * weight[:, None]).T
    return split_terms(analysis) + split_terms(synthesis)


def spectrum_kernel(taps_ref, high_ref, low_ref, out_ref):
    half = taps_ref.shape[0] // 2
    sums = jnp.dot(high_ref[...], taps_ref[...], preferred_element_type=F32)
    sums += jnp.dot(low_ref[...], taps_ref[...], preferred_element_type=F32)
    cosines, sines = sums[:half], sums[half:]
    first = lax.broadcasted_iota(jnp.int32, cosines.shape, 0) == 0
    out_ref[0] = cosines
    out_ref[1] = jnp.where(first, 0.0, sines)
    out_ref[2] = jnp.where(first, sines, cosines)


def filtered(signal, spectrum, tables):
    half = spectrum.shape[1]
    analysis_high, analysis_low, synthesis_high, synthesis_low = (t[...] for t in tables)
    coef = jnp.dot(analysis_high, signal, preferred_element_type=F32)
    coef += jnp.dot(analysis_low, signal, preferred_element_type=F32)
    cos_part, sin_part = coef[:half], coef[half:]
    keep, turn, other = (jnp.concatenate([spectrum[n]] * (signal.shape[1] // TILE), axis=1) for n in range(3))
    product = jnp.concatenate([cos_part * keep - sin_part * turn, sin_part * other + cos_part * turn], axis=0)
    high = product.astype(BF16)
    low = (product - high.astype(F32)).astype(BF16)
    result = jnp.dot(synthesis_high, high, preferred_element_type=F32)
    result += jnp.dot(synthesis_low, high, preferred_element_type=F32)
    result += jnp.dot(synthesis_high, low, preferred_element_type=F32)
    return result


class Cut:
    def __init__(self, frames, rows, width, tm, height):
        self.frames, self.rows, self.width, self.tm, self.height = frames, rows, width, tm, height
        self.devices = tm * height
        self.own = width // self.devices
        self.block = TILE // self.own
        self.frame_blocks, self.row_blocks = frames // self.block, rows // self.block
        self.tiles = width // TILE
        self.piece = (self.frame_blocks, rows, TILE)

    @staticmethod
    def fits(frames, rows, lanes, tm, height):
        own = lanes // PARTS // (tm * height)
        if own == 0 or TILE % own or lanes != PARTS * own * tm * height or lanes // PARTS % TILE:
            return False
        block = TILE // own
        return frames % block == 0 and rows % block == 0 and rows % 16 == 0 and rows // block % 2 == 0 and block % 8 == 0


def call(kernel, ins, outs, scratch=(), flops=0, held=None, dtype=BF16, vmem=VMEM_BYTES):
    unread = [] if held is None else [held]

    def body(*refs):
        kernel(*refs[: len(ins)], *refs[len(ins) + len(unread) :])

    moved = 2 * sum(int(np.prod(a.shape)) for a, _ in ins) + 2 * sum(int(np.prod(s)) for s, _ in outs)
    return pl.pallas_call(
        body,
        grid=(1,),
        in_specs=[spec for _, spec in ins] + [ANYWHERE] * len(unread),
        out_specs=[spec for _, spec in outs],
        out_shape=[jax.ShapeDtypeStruct(shape, dtype) for shape, _ in outs],
        scratch_shapes=list(scratch),
        input_output_aliases={} if held is None else {len(ins): 0},
        compiler_params=pltpu.CompilerParams(vmem_limit_bytes=vmem),
        cost_estimate=pl.CostEstimate(flops=flops, bytes_accessed=moved, transcendentals=0),
    )(*[array for array, _ in ins], *unread)


def whole(table):
    return table, pl.BlockSpec(table.shape, lambda n: (0,) * table.ndim)


def start_all(copies):
    for copy in copies:
        copy.start()
    return copies


def wait_all(copies):
    for copy in copies:
        copy.wait()


def load(pairs, sems, first=0):
    return start_all([pltpu.make_async_copy(a, b, sems.at[first + n]) for n, (a, b) in enumerate(pairs)])


def frame_runs(cut):
    step = cut.frames // steps_of(cut.frames, 16)
    return [pl.ds(first, step) for first in range(0, cut.frames, step)]


def shuffle_table(cut):
    count = cut.block * TILE
    n, m, lane = np.meshgrid(np.arange(cut.block), np.arange(cut.block), np.arange(cut.own), indexing="ij")
    table = np.zeros((count, count), np.float32)
    table[n * TILE + m * cut.own + lane, m * TILE + n * cut.own + lane] = 1
    return table.astype(jnp.bfloat16)


def shuffled(tiles, shuffle):
    moved = jnp.dot(jnp.concatenate(tiles, axis=1), shuffle[...], preferred_element_type=F32)
    return [moved[:, m * TILE : (m + 1) * TILE] for m in range(len(tiles))]


def pack_kernel(lane, cut, x_ref, shuffle_ref, out_ref, x_buf, shuffle, out_buf, sems):
    split = (cut.frame_blocks, cut.block, cut.rows, TILE)
    tiles = [pl.ds(lane + tile * TILE, TILE) for tile in range(cut.tiles)]
    arriving = load([(x_ref.at[:, :, at], x_buf.at[tile]) for tile, at in enumerate(tiles)], sems)
    (table,) = load([(shuffle_ref, shuffle)], sems, 2 * cut.tiles)
    leaving = []
    for tile in range(cut.tiles):
        arriving[tile].wait()
        x = x_buf[tile].reshape(split)
        if tile == 0:
            table.wait()
        moved = shuffled([x[:, n].reshape(-1, TILE) for n in range(cut.block)], shuffle)
        for n, piece in enumerate(moved):
            out_buf[tile * cut.block + n] = piece.astype(BF16).reshape(cut.piece)
        part = pl.ds(tile * cut.block, cut.block)
        leaving += load([(out_buf.at[part], out_ref.at[part])], sems, cut.tiles + tile)
    wait_all(leaving)


def unpack_add_kernel(lane, cut, y_ref, x_ref, shuffle_ref, out_ref, y_buf, x_buf, shuffle, sems):
    tiles = [pl.ds(lane + tile * TILE, TILE) for tile in range(cut.tiles)]
    parts = [pl.ds(tile * cut.block, cut.block) for tile in range(cut.tiles)]
    (table,) = load([(shuffle_ref, shuffle)], sems, 3 * cut.tiles)
    arriving = load([(y_ref.at[part], y_buf.at[part]) for part in parts], sems)
    added = load([(x_ref.at[:, :, at], x_buf.at[tile]) for tile, at in enumerate(tiles)], sems, cut.tiles)
    table.wait()
    leaving = []
    for tile in range(cut.tiles):
        arriving[tile].wait()
        moved = shuffled([y_buf[tile * cut.block + n].reshape(-1, TILE) for n in range(cut.block)], shuffle)
        added[tile].wait()
        for n, rows in enumerate(moved):
            rows = rows.reshape(cut.piece)
            for block in range(cut.frame_blocks):
                frame = block * cut.block + n
                x_buf[tile, frame] = (x_buf[tile, frame].astype(F32) + rows[block]).astype(BF16)
        leaving += load([(x_buf.at[tile], out_ref.at[:, :, tiles[tile]])], sems, 2 * cut.tiles + tile)
    wait_all(leaving)


def filter_kernel(cut, x_ref, spectrum_ref, analysis_h, analysis_l, synthesis_h, synthesis_l, rows_ref, shuffle_ref, *refs):
    out_ref, x_buf, temporal, wide, column, spectrum, *tables, row_table, shuffle, sems = refs
    every = cut.height * cut.row_blocks
    frame_blocks = cut.tm * cut.frame_blocks
    arriving = load([(x_ref, x_buf), (shuffle_ref, shuffle), (spectrum_ref, spectrum)], sems)
    arriving += load(zip((analysis_h, analysis_l, synthesis_h, synthesis_l), tables), sems, 3)
    (rows_table,) = load([(rows_ref, row_table)], sems, 3 + len(tables))
    wait_all(arriving)

    def block_rows(n):
        return pl.ds(n, frame_blocks, stride=cut.rows)

    def block_frames(n):
        return pl.ds(n, frame_blocks, stride=cut.block)

    for j in range(cut.height):
        for i in range(cut.tm):
            piece = x_buf[i * cut.height + j].astype(F32).reshape(-1, TILE)
            wide[i * piece.shape[0] : (i + 1) * piece.shape[0], :] = piece
        parts = [
            jnp.concatenate(
                [wide[block_rows(block * cut.block + n), :].astype(BF16) for block in range(cut.row_blocks)], axis=0
            )
            for n in range(cut.block)
        ]
        moved = shuffled(parts, shuffle)
        for block in range(cut.row_blocks):
            for n in range(cut.block):
                column[block, block_frames(n), :] = moved[n][block * frame_blocks : (block + 1) * frame_blocks]
        for block in range(0, cut.row_blocks, 2):
            signal = jnp.concatenate([column[block].astype(BF16), column[block + 1].astype(BF16)], axis=1)
            at = (j * cut.row_blocks + block) * TILE
            temporal[:, at : at + WIDE] = filtered(signal, spectrum[...], tables).astype(BF16)
    rows_table.wait()
    pairs = every // 2
    leaving = []
    for j in range(cut.height):
        for block in range(0, cut.row_blocks, 2):
            n = (j * cut.row_blocks + block) // 2
            matrix = row_table[(pairs - 1 - n) * WIDE : (2 * pairs - 1 - n) * WIDE, :]
            result = jnp.dot(temporal[...], matrix, preferred_element_type=F32)
            column[block], column[block + 1] = result[:, :TILE], result[:, TILE:]
        parts = [
            jnp.concatenate([column[block, block_frames(n), :].astype(BF16) for block in range(cut.row_blocks)], axis=0)
            for n in range(cut.block)
        ]
        moved = shuffled(parts, shuffle)
        for block in range(cut.row_blocks):
            for n in range(cut.block):
                rows = moved[n][block * frame_blocks : (block + 1) * frame_blocks]
                wide[block_rows(block * cut.block + n), :] = rows
        for i in range(cut.tm):
            count = cut.frame_blocks * cut.rows
            piece = wide[i * count : (i + 1) * count, :].astype(BF16).reshape(cut.piece)
            x_buf[i * cut.height + j] = piece
    wait_all(load([(x_buf, out_ref)], sems))


def row_matrices(cut, taps):
    size, own = taps.shape
    near = WIDE // own
    pairs = size // near
    far = np.arange(2 * pairs - 1)[:, None, None]
    source, target = np.arange(near)[None, :, None], np.arange(near)[None, None, :]
    index = ((2 * pairs - 1 - far - pairs) * near + target - source) % size
    chosen = (index.reshape(-1, 1) == np.arange(size)[None, :]).astype(jnp.bfloat16)
    picked = jnp.dot(chosen, taps, preferred_element_type=F32).astype(BF16)
    picked = picked.reshape((2 * pairs - 1) * near, 1, WIDE)
    same = jnp.asarray(np.tile(np.eye(own), (1, near)).astype(jnp.bfloat16))
    return (picked * same[None]).reshape((2 * pairs - 1) * WIDE, WIDE)


def shards(frames_in, time_taps, row_taps):
    frames, rows, lanes = frames_in.shape
    tm, height = lax.axis_size("tm"), lax.axis_size("height")
    if not Cut.fits(frames, rows, lanes, tm, height):
        return narrow_shards(frames_in, time_taps, row_taps)
    width = lanes // PARTS
    cut = Cut(frames, rows, width, tm, height)
    size = frames * tm
    tables, shuffle = fourier_tables(size), jnp.asarray(shuffle_table(cut))
    device = lax.axis_index("tm") * height + lax.axis_index("height")

    def free(*arrays):
        return [(array, ANYWHERE) for array in arrays]

    shape = (cut.devices,) + cut.piece
    sems = pltpu.SemaphoreType.DMA((3 * cut.tiles + 8,))
    tile_buf, table_buf = pltpu.VMEM((cut.tiles, frames, rows, TILE), BF16), pltpu.VMEM(shuffle.shape, BF16)
    piece_buf = pltpu.VMEM(shape, BF16)

    def exchange(pieces):
        flat = pieces.reshape(cut.devices, -1, TILE)
        return lax.all_to_all(flat, ("tm", "height"), 0, 0, tiled=True).reshape(shape)

    def pack(part):
        kernel = functools.partial(pack_kernel, part * width, cut)
        scratch = [tile_buf, table_buf, piece_buf, sems]
        return exchange(call(kernel, free(frames_in, shuffle), free(shape), scratch)[0])

    def own_lanes(taps, part):
        first = (part * width + device * cut.own) % taps.shape[1]
        return lax.dynamic_slice_in_dim(taps, first, cut.own, axis=1)

    def both(pieces, part):
        taps = jnp.tile(own_lanes(time_taps, part), (1, TILE // cut.own))
        out = ((3, size // 2, TILE), pl.BlockSpec((3, size // 2, TILE), lambda n: (0, 0, 0)))
        (spectrum,) = call(spectrum_kernel, [whole(t) for t in (taps, *tables[:2])], [out], dtype=F32, vmem=FILTER_VMEM)
        matrices = row_matrices(cut, own_lanes(row_taps, part))
        every = rows * height * cut.own
        scratch = [piece_buf, pltpu.VMEM((size, every), BF16), pltpu.VMEM((size // cut.block * rows, TILE), F32)]
        scratch += [pltpu.VMEM((cut.row_blocks, size, TILE), F32), pltpu.VMEM(spectrum.shape, F32)]
        scratch += [pltpu.VMEM(t.shape, BF16) for t in (*tables, matrices, shuffle)] + [sems]
        ins = free(pieces, spectrum, *tables, matrices, shuffle)
        flops = 2 * size * every * (5 * size + every)
        return exchange(call(functools.partial(filter_kernel, cut), ins, free(shape), scratch, flops, vmem=FILTER_VMEM)[0])

    def unpack_add(pieces, part, held):
        kernel = functools.partial(unpack_add_kernel, part * width, cut)
        scratch = [piece_buf, tile_buf, table_buf, sems]
        return call(kernel, free(pieces, frames_in, shuffle), free(frames_in.shape), scratch, held=held)[0]

    arrived = [pack(part) for part in range(PARTS)]
    returned = [both(pieces, part) for part, pieces in enumerate(arrived)]
    out = None
    for part, pieces in enumerate(returned):
        out = unpack_add(pieces, part, out)
    return out


def lane_taps(tap_table, first_lane, lane_count):
    channels = tap_table.shape[1]
    distinct = min(lane_count, channels)
    lane_ids = (first_lane + lax.iota(jnp.int32, distinct)) % channels
    selector = (lane_ids[None, :] == lax.iota(jnp.int32, channels)[:, None]).astype(tap_table.dtype)
    picked = jnp.dot(tap_table, selector, preferred_element_type=jnp.float32).astype(
        tap_table.dtype
    )
    return jnp.transpose(picked)


def shifted_taps(taps, base, size):
    distinct, period = taps.shape
    start = (base - (size - 1)) % period
    tiled = jnp.concatenate([taps, taps, taps], axis=1)
    window = lax.slice_in_dim(tiled, start, start + 2 * size - 1, axis=1)
    reversed_window = window[:, ::-1]
    padded = jnp.concatenate([reversed_window, jnp.zeros((distinct, 1), taps.dtype)], axis=1)
    repeated = jnp.tile(padded, (1, size + 1))
    flat = lax.slice_in_dim(repeated, size - 1, size - 1 + size * (2 * size - 1), axis=1)
    return flat.reshape(distinct, size, 2 * size - 1)[:, :, :size]


def time_convolve(segment, own_taps):
    frames, rows_here, lane_count = segment.shape
    distinct = own_taps.shape[0]
    columns = lane_count // distinct
    block_len = min(128, frames)
    block_count = frames // block_len
    blocked = segment.reshape(block_count, block_len, rows_here, columns, distinct)
    blocked = jnp.transpose(blocked, (4, 3, 2, 0, 1))
    running = jnp.zeros((distinct, columns, rows_here, block_count, block_len), jnp.float32)
    for lag_index in range(block_count):
        toeplitz = shifted_taps(own_taps, lag_index * block_len, block_len)
        rolled = jnp.roll(blocked, lag_index, axis=3)
        running = running + jnp.einsum(
            "cab,cxrnb->cxrna", toeplitz, rolled, preferred_element_type=jnp.float32
        )
    result = jnp.transpose(running, (3, 4, 2, 1, 0)).reshape(frames, rows_here, lane_count)
    return result.astype(jnp.bfloat16)


def row_convolve(segment, row_taps):
    frames, height, lane_count = segment.shape
    distinct = row_taps.shape[0]
    columns = lane_count // distinct
    arranged = jnp.transpose(segment.reshape(frames, height, columns, distinct), (3, 2, 0, 1))
    circulant = shifted_taps(row_taps, 0, height)
    filtered = jnp.einsum("cab,cxfb->cxfa", circulant, arranged, preferred_element_type=jnp.float32)
    result = jnp.transpose(filtered, (2, 3, 1, 0)).reshape(frames, height, lane_count)
    return result.astype(jnp.bfloat16)


def narrow_shards(frames_in, time_filter, height_filter):
    frames_dev, rows_dev, lane_total = frames_in.shape
    tm_count = lax.axis_size("tm")
    height_count = lax.axis_size("height")
    lane_count = lane_total // (tm_count * height_count)
    first_lane = (
        lax.axis_index("tm") * (lane_total // tm_count) + lax.axis_index("height") * lane_count
    )
    own_taps = lane_taps(time_filter, first_lane, lane_count)
    row_taps = lane_taps(height_filter, first_lane, lane_count)
    gathered = lax.all_to_all(
        lax.all_to_all(frames_in, "tm", split_axis=2, concat_axis=0, tiled=True),
        "height",
        split_axis=2,
        concat_axis=1,
        tiled=True,
    )
    temporal = time_convolve(gathered, own_taps)
    spatial_lanes = row_convolve(temporal, row_taps)
    returned = lax.all_to_all(
        lax.all_to_all(spatial_lanes, "tm", split_axis=0, concat_axis=2, tiled=True),
        "height",
        split_axis=1,
        concat_axis=2,
        tiled=True,
    )
    spatial = returned.reshape(frames_dev, rows_dev, height_count, tm_count, lane_count)
    spatial = jnp.transpose(spatial, (0, 1, 3, 2, 4)).reshape(frames_dev, rows_dev, lane_total)
    return (frames_in.astype(jnp.float32) + spatial.astype(jnp.float32)).astype(jnp.bfloat16)


def solution(mesh):
    return jax.shard_map(
        shards,
        mesh=mesh,
        in_specs=(P("tm", "height", None), P(), P()),
        out_specs=P("tm", "height", None),
        check_vma=False,
    )
```

```python
import functools

import jax
import jax.numpy as jnp
import numpy as np
from jax import lax
from jax.experimental import pallas as pl
from jax.experimental.pallas import tpu as pltpu
from jax.sharding import PartitionSpec as P

F32, BF16 = jnp.float32, jnp.bfloat16
TILE = 128
WIDE = 2 * TILE
PARTS = 2
VMEM_BYTES = 62 << 20
FILTER_VMEM = 40 << 20
RUNS = 2
ANYWHERE = pl.BlockSpec(memory_space=pl.ANY)


def split_terms(table):
    high = table.astype(jnp.bfloat16)
    low = (table - high.astype(np.float64)).astype(jnp.bfloat16)
    return high, low


def fourier_tables(size):
    half = size // 2
    wave, at = np.arange(half)[:, None], np.arange(size)[None, :]
    angle = 2.0 * np.pi * ((wave * at) % size) / size
    sines = np.sin(angle)
    sines[0] = 1.0 - 2.0 * (np.arange(size) % 2)
    analysis = np.concatenate([np.cos(angle), sines], axis=0)
    weight = np.full((size,), 2.0 / size)
    weight[0] = weight[half] = 1.0 / size
    synthesis = (analysis * weight[:, None]).T
    return split_terms(analysis) + split_terms(synthesis)


def spectrum_kernel(taps_ref, high_ref, low_ref, out_ref):
    half = taps_ref.shape[0] // 2
    sums = jnp.dot(high_ref[...], taps_ref[...], preferred_element_type=F32)
    sums += jnp.dot(low_ref[...], taps_ref[...], preferred_element_type=F32)
    cosines, sines = sums[:half], sums[half:]
    first = lax.broadcasted_iota(jnp.int32, cosines.shape, 0) == 0
    out_ref[0] = cosines
    out_ref[1] = jnp.where(first, 0.0, sines)
    out_ref[2] = jnp.where(first, sines, cosines)


def filtered(signal, spectrum, tables):
    half = spectrum.shape[1]
    analysis_high, analysis_low, synthesis_high, synthesis_low = (t[...] for t in tables)
    coef = jnp.dot(analysis_high, signal, preferred_element_type=F32)
    coef += jnp.dot(analysis_low, signal, preferred_element_type=F32)
    cos_part, sin_part = coef[:half], coef[half:]
    keep, turn, other = (jnp.concatenate([spectrum[n]] * (signal.shape[1] // TILE), axis=1) for n in range(3))
    product = jnp.concatenate([cos_part * keep - sin_part * turn, sin_part * other + cos_part * turn], axis=0)
    high = product.astype(BF16)
    low = (product - high.astype(F32)).astype(BF16)
    result = jnp.dot(synthesis_high, high, preferred_element_type=F32)
    result += jnp.dot(synthesis_low, high, preferred_element_type=F32)
    result += jnp.dot(synthesis_high, low, preferred_element_type=F32)
    return result


class Cut:
    def __init__(self, frames, rows, width, tm, height):
        self.frames, self.rows, self.width, self.tm, self.height = frames, rows, width, tm, height
        self.devices = tm * height
        self.own = width // self.devices
        self.block = TILE // self.own
        self.frame_blocks, self.row_blocks = frames // self.block, rows // self.block
        self.tiles = width // TILE
        self.piece = (self.frame_blocks, rows, TILE)

    @staticmethod
    def fits(frames, rows, lanes, tm, height):
        own = lanes // PARTS // (tm * height)
        if own == 0 or TILE % own or lanes != PARTS * own * tm * height or lanes // PARTS % TILE:
            return False
        block = TILE // own
        return frames % block == 0 and rows % block == 0 and rows % 16 == 0 and rows // block % 2 == 0 and block % 8 == 0


def call(kernel, ins, outs, scratch=(), flops=0, held=None, dtype=BF16, vmem=VMEM_BYTES):
    unread = [] if held is None else [held]

    def body(*refs):
        kernel(*refs[: len(ins)], *refs[len(ins) + len(unread) :])

    moved = 2 * sum(int(np.prod(a.shape)) for a, _ in ins) + 2 * sum(int(np.prod(s)) for s, _ in outs)
    return pl.pallas_call(
        body,
        grid=(1,),
        in_specs=[spec for _, spec in ins] + [ANYWHERE] * len(unread),
        out_specs=[spec for _, spec in outs],
        out_shape=[jax.ShapeDtypeStruct(shape, dtype) for shape, _ in outs],
        scratch_shapes=list(scratch),
        input_output_aliases={} if held is None else {len(ins): 0},
        compiler_params=pltpu.CompilerParams(vmem_limit_bytes=vmem),
        cost_estimate=pl.CostEstimate(flops=flops, bytes_accessed=moved, transcendentals=0),
    )(*[array for array, _ in ins], *unread)


def whole(table):
    return table, pl.BlockSpec(table.shape, lambda n: (0,) * table.ndim)


def start_all(copies):
    for copy in copies:
        copy.start()
    return copies


def wait_all(copies):
    for copy in copies:
        copy.wait()


def load(pairs, sems, first=0):
    return start_all([pltpu.make_async_copy(a, b, sems.at[first + n]) for n, (a, b) in enumerate(pairs)])


def frame_runs(cut):
    step = cut.frames // steps_of(cut.frames, 16)
    return [pl.ds(first, step) for first in range(0, cut.frames, step)]


def fill_shuffle(cut, shuffle):
    shape = shuffle.shape
    row, column = (lax.broadcasted_iota(jnp.int32, shape, axis) for axis in range(2))
    m, n, lane = column // TILE, column % TILE // cut.own, column % cut.own
    shuffle[...] = (row == n * TILE + m * cut.own + lane).astype(F32).astype(BF16)


def shuffled(tiles, shuffle):
    moved = jnp.dot(jnp.concatenate(tiles, axis=1), shuffle[...], preferred_element_type=F32)
    return [moved[:, m * TILE : (m + 1) * TILE] for m in range(len(tiles))]


def in_turn(cut):
    count = next(n for n in (RUNS, 1) if cut.frame_blocks % n == 0)
    step = cut.frame_blocks // count
    return step, range(0, cut.frame_blocks, step), range(0, cut.block, 2)


def exchange_lanes(cut, step, lhs, shuffle, first):
    columns = slice(first * TILE, (first + 2) * TILE)
    moved = jnp.dot(lhs[...], shuffle[:, columns], preferred_element_type=F32)
    shape = (cut.tiles, step, cut.rows, TILE)
    return [(first + n, moved[:, n * TILE : (n + 1) * TILE].reshape(shape)) for n in range(2)]


def pack_kernel(lane, cut, x_ref, out_ref, x_buf, shuffle, lhs, out_buf, sems):
    step, runs, pairs = in_turn(cut)
    size = step * cut.rows
    frames = [pl.ds(run * cut.block, step * cut.block) for run in runs]
    arriving = load([(x_ref.at[at, :, pl.ds(lane, cut.width)], x_buf.at[at]) for at in frames], sems)
    fill_shuffle(cut, shuffle)
    leaving = []
    for turn, run in enumerate(runs):
        arriving[turn].wait()
        for tile in range(cut.tiles):
            lanes = slice(tile * TILE, (tile + 1) * TILE)
            x = x_buf[frames[turn], :, lanes].reshape(step, cut.block, cut.rows, TILE)
            for n in range(cut.block):
                lhs[tile * size : (tile + 1) * size, n * TILE : (n + 1) * TILE] = x[:, n].reshape(size, TILE)
        for pair in pairs:
            for m, piece in exchange_lanes(cut, step, lhs, shuffle, pair):
                for tile in range(cut.tiles):
                    out_buf[m * cut.tiles + tile, run : run + step] = piece[tile].astype(BF16)
            some = (pl.ds(pair * cut.tiles, 2 * cut.tiles), pl.ds(run, step))
            leaving += load([(out_buf.at[some], out_ref.at[some])], sems, len(runs) + len(leaving))
    wait_all(leaving)


def unpack_add_kernel(lane, cut, y_ref, x_ref, out_ref, y_buf, x_buf, shuffle, lhs, sems):
    step, runs, pairs = in_turn(cut)
    size = step * cut.rows
    lanes = pl.ds(lane, cut.width)
    parts = [pl.ds(run, step) for run in runs]
    frames = [pl.ds(run * cut.block, step * cut.block) for run in runs]
    arriving, added = [], []
    for turn, (part, at) in enumerate(zip(parts, frames)):
        arriving += load([(y_ref.at[:, part], y_buf.at[:, part])], sems, turn)
        added += load([(x_ref.at[at, :, lanes], x_buf.at[at])], sems, RUNS + turn)
    fill_shuffle(cut, shuffle)
    leaving = []
    for turn, run in enumerate(runs):
        arriving[turn].wait()
        for tile in range(cut.tiles):
            for m in range(cut.block):
                piece = y_buf[m * cut.tiles + tile, run : run + step].reshape(size, TILE)
                lhs[tile * size : (tile + 1) * size, m * TILE : (m + 1) * TILE] = piece
        added[turn].wait()
        for pair in pairs:
            for n, piece in exchange_lanes(cut, step, lhs, shuffle, pair):
                for tile in range(cut.tiles):
                    for block in range(step):
                        frame, at = (run + block) * cut.block + n, slice(tile * TILE, (tile + 1) * TILE)
                        x_buf[frame, :, at] = (x_buf[frame, :, at].astype(F32) + piece[tile, block]).astype(BF16)
        leaving += load([(x_buf.at[frames[turn]], out_ref.at[frames[turn], :, lanes])], sems, 2 * RUNS + turn)
    wait_all(leaving)


def filter_kernel(cut, x_ref, spectrum_ref, analysis_h, analysis_l, synthesis_h, synthesis_l, rows_ref, *refs):
    out_ref, x_buf, temporal, wide, column, spectrum, *tables, row_table, shuffle, sems = refs
    every = cut.height * cut.row_blocks
    frame_blocks = cut.tm * cut.frame_blocks
    arriving = load([(x_ref, x_buf), (spectrum_ref, spectrum)], sems)
    arriving += load(zip((analysis_h, analysis_l, synthesis_h, synthesis_l), tables), sems, 2)
    (rows_table,) = load([(rows_ref, row_table)], sems, 2 + len(tables))
    fill_shuffle(cut, shuffle)
    wait_all(arriving)

    def block_rows(n):
        return pl.ds(n, frame_blocks, stride=cut.rows)

    def block_frames(n):
        return pl.ds(n, frame_blocks, stride=cut.block)

    def along_time(j, _):
        for i in range(cut.tm):
            piece = x_buf[i * cut.height + j].astype(F32).reshape(-1, TILE)
            wide[i * piece.shape[0] : (i + 1) * piece.shape[0], :] = piece
        parts = [
            jnp.concatenate(
                [wide[block_rows(block * cut.block + n), :].astype(BF16) for block in range(cut.row_blocks)], axis=0
            )
            for n in range(cut.block)
        ]
        moved = shuffled(parts, shuffle)
        for block in range(cut.row_blocks):
            for n in range(cut.block):
                column[block, block_frames(n), :] = moved[n][block * frame_blocks : (block + 1) * frame_blocks]
        for block in range(0, cut.row_blocks, 2):
            signal = jnp.concatenate([column[block].astype(BF16), column[block + 1].astype(BF16)], axis=1)
            at = pl.ds(pl.multiple_of((j * cut.row_blocks + block) * TILE, WIDE), WIDE)
            temporal[:, at] = filtered(signal, spectrum[...], tables).astype(BF16)
        return _

    def along_rows(j, _):
        for block in range(0, cut.row_blocks, 2):
            first = pairs - 1 - (j * cut.row_blocks + block) // 2
            matrix = row_table[pl.ds(pl.multiple_of(first * WIDE, WIDE), pairs * WIDE), :]
            result = jnp.dot(temporal[...], matrix, preferred_element_type=F32)
            column[block], column[block + 1] = result[:, :TILE], result[:, TILE:]
        parts = [
            jnp.concatenate([column[block, block_frames(n), :].astype(BF16) for block in range(cut.row_blocks)], axis=0)
            for n in range(cut.block)
        ]
        moved = shuffled(parts, shuffle)
        for block in range(cut.row_blocks):
            for n in range(cut.block):
                rows = moved[n][block * frame_blocks : (block + 1) * frame_blocks]
                wide[block_rows(block * cut.block + n), :] = rows
        for i in range(cut.tm):
            count = cut.frame_blocks * cut.rows
            x_buf[i * cut.height + j] = wide[i * count : (i + 1) * count, :].astype(BF16).reshape(cut.piece)
        return _

    pairs = every // 2
    lax.fori_loop(0, cut.height, along_time, 0)
    rows_table.wait()
    lax.fori_loop(0, cut.height, along_rows, 0)
    wait_all(load([(x_buf, out_ref)], sems))


def row_matrices(cut, taps):
    size, own = taps.shape
    near = WIDE // own
    pairs = size // near
    far = np.arange(2 * pairs - 1)[:, None, None]
    source, target = np.arange(near)[None, :, None], np.arange(near)[None, None, :]
    index = ((2 * pairs - 1 - far - pairs) * near + target - source) % size
    chosen = (index.reshape(-1, 1) == np.arange(size)[None, :]).astype(jnp.bfloat16)
    picked = jnp.dot(chosen, taps, preferred_element_type=F32).astype(BF16)
    picked = picked.reshape((2 * pairs - 1) * near, 1, WIDE)
    same = jnp.asarray(np.tile(np.eye(own), (1, near)).astype(jnp.bfloat16))
    return (picked * same[None]).reshape((2 * pairs - 1) * WIDE, WIDE)


def shards(frames_in, time_taps, row_taps):
    frames, rows, lanes = frames_in.shape
    tm, height = lax.axis_size("tm"), lax.axis_size("height")
    if not Cut.fits(frames, rows, lanes, tm, height):
        return narrow_shards(frames_in, time_taps, row_taps)
    width = lanes // PARTS
    cut = Cut(frames, rows, width, tm, height)
    size = frames * tm
    tables = fourier_tables(size)
    device = lax.axis_index("tm") * height + lax.axis_index("height")

    def free(*arrays):
        return [(array, ANYWHERE) for array in arrays]

    shape = (cut.devices,) + cut.piece
    sems = pltpu.SemaphoreType.DMA((RUNS * (cut.block // 2 + 2) + 8,))
    part_buf, table_buf = pltpu.VMEM((frames, rows, width), BF16), pltpu.VMEM((cut.block * TILE,) * 2, BF16)
    piece_buf = pltpu.VMEM(shape, BF16)
    lhs = pltpu.VMEM((cut.tiles * in_turn(cut)[0] * rows, cut.block * TILE), BF16)

    def exchange(pieces):
        flat = pieces.reshape(cut.devices, -1, TILE)
        return lax.all_to_all(flat, ("tm", "height"), 0, 0, tiled=True).reshape(shape)

    def pack(part):
        kernel = functools.partial(pack_kernel, part * width, cut)
        scratch = [part_buf, table_buf, lhs, piece_buf, sems]
        return exchange(call(kernel, free(frames_in), free(shape), scratch)[0])

    def own_lanes(taps, part):
        first = (part * width + device % cut.tiles * TILE + device // cut.tiles * cut.own) % taps.shape[1]
        return lax.dynamic_slice_in_dim(taps, first, cut.own, axis=1)

    def both(pieces, part):
        taps = jnp.tile(own_lanes(time_taps, part), (1, TILE // cut.own))
        out = ((3, size // 2, TILE), pl.BlockSpec((3, size // 2, TILE), lambda n: (0, 0, 0)))
        (spectrum,) = call(spectrum_kernel, [whole(t) for t in (taps, *tables[:2])], [out], dtype=F32, vmem=FILTER_VMEM)
        matrices = row_matrices(cut, own_lanes(row_taps, part))
        every = rows * height * cut.own
        scratch = [piece_buf, pltpu.VMEM((size, every), BF16), pltpu.VMEM((size // cut.block * rows, TILE), F32)]
        scratch += [pltpu.VMEM((cut.row_blocks, size, TILE), F32), pltpu.VMEM(spectrum.shape, F32)]
        scratch += [pltpu.VMEM(t.shape, BF16) for t in (*tables, matrices)] + [table_buf, sems]
        ins = free(pieces, spectrum, *tables, matrices)
        flops = 2 * size * every * (5 * size + every)
        return exchange(call(functools.partial(filter_kernel, cut), ins, free(shape), scratch, flops, vmem=FILTER_VMEM)[0])

    def unpack_add(pieces, part, held):
        kernel = functools.partial(unpack_add_kernel, part * width, cut)
        scratch = [piece_buf, part_buf, table_buf, lhs, sems]
        return call(kernel, free(pieces, frames_in), free(frames_in.shape), scratch, held=held)[0]

    arrived = [pack(part) for part in range(PARTS)]
    returned = [both(pieces, part) for part, pieces in enumerate(arrived)]
    out = None
    for part, pieces in enumerate(returned):
        out = unpack_add(pieces, part, out)
    return out


def lane_taps(tap_table, first_lane, lane_count):
    channels = tap_table.shape[1]
    distinct = min(lane_count, channels)
    lane_ids = (first_lane + lax.iota(jnp.int32, distinct)) % channels
    selector = (lane_ids[None, :] == lax.iota(jnp.int32, channels)[:, None]).astype(tap_table.dtype)
    picked = jnp.dot(tap_table, selector, preferred_element_type=jnp.float32).astype(
        tap_table.dtype
    )
    return jnp.transpose(picked)


def shifted_taps(taps, base, size):
    distinct, period = taps.shape
    start = (base - (size - 1)) % period
    tiled = jnp.concatenate([taps, taps, taps], axis=1)
    window = lax.slice_in_dim(tiled, start, start + 2 * size - 1, axis=1)
    reversed_window = window[:, ::-1]
    padded = jnp.concatenate([reversed_window, jnp.zeros((distinct, 1), taps.dtype)], axis=1)
    repeated = jnp.tile(padded, (1, size + 1))
    flat = lax.slice_in_dim(repeated, size - 1, size - 1 + size * (2 * size - 1), axis=1)
    return flat.reshape(distinct, size, 2 * size - 1)[:, :, :size]


def time_convolve(segment, own_taps):
    frames, rows_here, lane_count = segment.shape
    distinct = own_taps.shape[0]
    columns = lane_count // distinct
    block_len = min(128, frames)
    block_count = frames // block_len
    blocked = segment.reshape(block_count, block_len, rows_here, columns, distinct)
    blocked = jnp.transpose(blocked, (4, 3, 2, 0, 1))
    running = jnp.zeros((distinct, columns, rows_here, block_count, block_len), jnp.float32)
    for lag_index in range(block_count):
        toeplitz = shifted_taps(own_taps, lag_index * block_len, block_len)
        rolled = jnp.roll(blocked, lag_index, axis=3)
        running = running + jnp.einsum(
            "cab,cxrnb->cxrna", toeplitz, rolled, preferred_element_type=jnp.float32
        )
    result = jnp.transpose(running, (3, 4, 2, 1, 0)).reshape(frames, rows_here, lane_count)
    return result.astype(jnp.bfloat16)


def row_convolve(segment, row_taps):
    frames, height, lane_count = segment.shape
    distinct = row_taps.shape[0]
    columns = lane_count // distinct
    arranged = jnp.transpose(segment.reshape(frames, height, columns, distinct), (3, 2, 0, 1))
    circulant = shifted_taps(row_taps, 0, height)
    filtered = jnp.einsum("cab,cxfb->cxfa", circulant, arranged, preferred_element_type=jnp.float32)
    result = jnp.transpose(filtered, (2, 3, 1, 0)).reshape(frames, height, lane_count)
    return result.astype(jnp.bfloat16)


def narrow_shards(frames_in, time_filter, height_filter):
    frames_dev, rows_dev, lane_total = frames_in.shape
    tm_count = lax.axis_size("tm")
    height_count = lax.axis_size("height")
    lane_count = lane_total // (tm_count * height_count)
    first_lane = (
        lax.axis_index("tm") * (lane_total // tm_count) + lax.axis_index("height") * lane_count
    )
    own_taps = lane_taps(time_filter, first_lane, lane_count)
    row_taps = lane_taps(height_filter, first_lane, lane_count)
    gathered = lax.all_to_all(
        lax.all_to_all(frames_in, "tm", split_axis=2, concat_axis=0, tiled=True),
        "height",
        split_axis=2,
        concat_axis=1,
        tiled=True,
    )
    temporal = time_convolve(gathered, own_taps)
    spatial_lanes = row_convolve(temporal, row_taps)
    returned = lax.all_to_all(
        lax.all_to_all(spatial_lanes, "tm", split_axis=0, concat_axis=2, tiled=True),
        "height",
        split_axis=1,
        concat_axis=2,
        tiled=True,
    )
    spatial = returned.reshape(frames_dev, rows_dev, height_count, tm_count, lane_count)
    spatial = jnp.transpose(spatial, (0, 1, 3, 2, 4)).reshape(frames_dev, rows_dev, lane_total)
    return (frames_in.astype(jnp.float32) + spatial.astype(jnp.float32)).astype(jnp.bfloat16)


def solution(mesh):
    return jax.shard_map(
        shards,
        mesh=mesh,
        in_specs=(P("tm", "height", None), P(), P()),
        out_specs=P("tm", "height", None),
        check_vma=False,
    )
```

```python
import functools

import jax
import jax.numpy as jnp
import numpy as np
from jax import lax
from jax.experimental import pallas as pl
from jax.experimental.pallas import tpu as pltpu
from jax.sharding import PartitionSpec as P

F32, BF16 = jnp.float32, jnp.bfloat16
TILE = 128
WIDE = 2 * TILE
PARTS = 2
VMEM_BYTES = 62 << 20
FILTER_VMEM = 40 << 20
RUNS = 2
FOLDS = 2
ANYWHERE = pl.BlockSpec(memory_space=pl.ANY)


def split_terms(table):
    high = table.astype(jnp.bfloat16)
    low = (table - high.astype(np.float64)).astype(jnp.bfloat16)
    return high, low


def fourier_tables(size):
    half = size // 2
    wave, at = np.arange(half)[:, None], np.arange(size)[None, :]
    angle = 2.0 * np.pi * ((wave * at) % size) / size
    sines = np.sin(angle)
    sines[0] = 1.0 - 2.0 * (np.arange(size) % 2)
    analysis = np.concatenate([np.cos(angle), sines], axis=0)
    weight = np.full((size,), 2.0 / size)
    weight[0] = weight[half] = 1.0 / size
    synthesis = (analysis * weight[:, None]).T
    return split_terms(analysis) + split_terms(synthesis)


def spectrum_kernel(taps_ref, high_ref, low_ref, out_ref):
    half = taps_ref.shape[0] // 2
    sums = jnp.dot(high_ref[...], taps_ref[...], preferred_element_type=F32)
    sums += jnp.dot(low_ref[...], taps_ref[...], preferred_element_type=F32)
    cosines, sines = sums[:half], sums[half:]
    first = lax.broadcasted_iota(jnp.int32, cosines.shape, 0) == 0
    out_ref[0] = cosines
    out_ref[1] = jnp.where(first, 0.0, sines)
    out_ref[2] = jnp.where(first, sines, cosines)


def filtered(signal, spectrum, tables):
    half = spectrum.shape[1]
    analysis_high, analysis_low, synthesis_high, synthesis_low = (t[...] for t in tables)
    coef = jnp.dot(analysis_high, signal, preferred_element_type=F32)
    coef += jnp.dot(analysis_low, signal, preferred_element_type=F32)
    cos_part, sin_part = coef[:half], coef[half:]
    keep, turn, other = (jnp.concatenate([spectrum[n]] * (signal.shape[1] // TILE), axis=1) for n in range(3))
    product = jnp.concatenate([cos_part * keep - sin_part * turn, sin_part * other + cos_part * turn], axis=0)
    high = product.astype(BF16)
    low = (product - high.astype(F32)).astype(BF16)
    result = jnp.dot(synthesis_high, high, preferred_element_type=F32)
    result += jnp.dot(synthesis_low, high, preferred_element_type=F32)
    result += jnp.dot(synthesis_high, low, preferred_element_type=F32)
    return result


class Cut:
    def __init__(self, frames, rows, width, tm, height):
        self.frames, self.rows, self.width, self.tm, self.height = frames, rows, width, tm, height
        self.devices = tm * height
        self.own = width // self.devices
        self.block = TILE // self.own
        self.frame_blocks, self.row_blocks = frames // self.block, rows // self.block
        self.tiles = width // TILE
        self.piece = (self.frame_blocks, rows, TILE)

    @staticmethod
    def fits(frames, rows, lanes, channels, tm, height):
        own = lanes // PARTS // (tm * height)
        if own == 0 or TILE % own or lanes != PARTS * own * tm * height or lanes // PARTS % TILE or channels % own:
            return False
        block = TILE // own
        return frames % block == 0 and rows % block == 0 and rows % 16 == 0 and rows // block % 2 == 0 and block % (2 * FOLDS) == 0


def call(kernel, ins, outs, scratch=(), flops=0, held=None, dtype=BF16, vmem=VMEM_BYTES):
    unread = [] if held is None else [held]

    def body(*refs):
        kernel(*refs[: len(ins)], *refs[len(ins) + len(unread) :])

    moved = 2 * sum(int(np.prod(a.shape)) for a, _ in ins) + 2 * sum(int(np.prod(s)) for s, _ in outs)
    return pl.pallas_call(
        body,
        grid=(1,),
        in_specs=[spec for _, spec in ins] + [ANYWHERE] * len(unread),
        out_specs=[spec for _, spec in outs],
        out_shape=[jax.ShapeDtypeStruct(shape, dtype) for shape, _ in outs],
        scratch_shapes=list(scratch),
        input_output_aliases={} if held is None else {len(ins): 0},
        compiler_params=pltpu.CompilerParams(vmem_limit_bytes=vmem),
        cost_estimate=pl.CostEstimate(flops=flops, bytes_accessed=moved, transcendentals=0),
    )(*[array for array, _ in ins], *unread)


def whole(table):
    return table, pl.BlockSpec(table.shape, lambda n: (0,) * table.ndim)


def start_all(copies):
    for copy in copies:
        copy.start()
    return copies


def wait_all(copies):
    for copy in copies:
        copy.wait()


def load(pairs, sems, first=0):
    return start_all([pltpu.make_async_copy(a, b, sems.at[first + n]) for n, (a, b) in enumerate(pairs)])


def frame_runs(cut):
    step = cut.frames // steps_of(cut.frames, 16)
    return [pl.ds(first, step) for first in range(0, cut.frames, step)]


def fill_shuffle(cut, shuffle):
    shape = shuffle.shape
    row, column = (lax.broadcasted_iota(jnp.int32, shape, axis) for axis in range(2))
    m, n, lane = column // TILE, column % TILE // cut.own, column % cut.own
    shuffle[...] = (row == n * (TILE // FOLDS) + m * cut.own + lane).astype(F32).astype(BF16)


def folds(tiles):
    for fold in range(FOLDS):
        lanes = slice(fold * TILE // FOLDS, (fold + 1) * TILE // FOLDS)
        yield [
            jnp.concatenate([tile[:, lanes] for tile in tiles[n : n + FOLDS]], axis=1)
            for n in range(0, len(tiles), FOLDS)
        ]


def shuffled(tiles, shuffle):
    result = []
    for part in folds(tiles):
        moved = jnp.dot(jnp.concatenate(part, axis=1), shuffle[...], preferred_element_type=F32)
        result += [moved[:, m * TILE : (m + 1) * TILE] for m in range(len(tiles) // FOLDS)]
    return result


def lay_out(tiles, lhs, rows):
    for fold, part in enumerate(folds(tiles)):
        for n, tile in enumerate(part):
            lhs[fold, rows, n * TILE : (n + 1) * TILE] = tile


def in_turn(cut):
    count = next(n for n in (RUNS, 1) if cut.frame_blocks % n == 0)
    step = cut.frame_blocks // count
    return step, range(0, cut.frame_blocks, step), range(0, cut.block, 2)


def exchange_lanes(cut, step, lhs, shuffle, first):
    fold, at = divmod(first, cut.block // FOLDS)
    moved = jnp.dot(lhs[fold], shuffle[:, at * TILE : (at + 2) * TILE], preferred_element_type=F32)
    shape = (cut.tiles, step, cut.rows, TILE)
    return [(first + n, moved[:, n * TILE : (n + 1) * TILE].reshape(shape)) for n in range(2)]


def pack_kernel(lane, cut, x_ref, out_ref, x_buf, shuffle, lhs, out_buf, sems):
    step, runs, pairs = in_turn(cut)
    size = step * cut.rows
    frames = [pl.ds(run * cut.block, step * cut.block) for run in runs]
    arriving = load([(x_ref.at[at, :, pl.ds(lane, cut.width)], x_buf.at[at]) for at in frames], sems)
    fill_shuffle(cut, shuffle)
    leaving = []
    for turn, run in enumerate(runs):
        arriving[turn].wait()
        for tile in range(cut.tiles):
            lanes = slice(tile * TILE, (tile + 1) * TILE)
            x = x_buf[frames[turn], :, lanes].reshape(step, cut.block, cut.rows, TILE)
            lay_out([x[:, n].reshape(size, TILE) for n in range(cut.block)], lhs, slice(tile * size, (tile + 1) * size))
        for pair in pairs:
            for m, piece in exchange_lanes(cut, step, lhs, shuffle, pair):
                for tile in range(cut.tiles):
                    out_buf[m * cut.tiles + tile, run : run + step] = piece[tile].astype(BF16)
            some = (pl.ds(pair * cut.tiles, 2 * cut.tiles), pl.ds(run, step))
            leaving += load([(out_buf.at[some], out_ref.at[some])], sems, len(runs) + len(leaving))
    wait_all(leaving)


def unpack_add_kernel(lane, cut, y_ref, x_ref, out_ref, y_buf, x_buf, shuffle, lhs, sems):
    step, runs, pairs = in_turn(cut)
    size = step * cut.rows
    lanes = pl.ds(lane, cut.width)
    parts = [pl.ds(run, step) for run in runs]
    frames = [pl.ds(run * cut.block, step * cut.block) for run in runs]
    arriving, added = [], []
    for turn, (part, at) in enumerate(zip(parts, frames)):
        arriving += load([(y_ref.at[:, part], y_buf.at[:, part])], sems, turn)
        added += load([(x_ref.at[at, :, lanes], x_buf.at[at])], sems, RUNS + turn)
    fill_shuffle(cut, shuffle)
    leaving = []
    for turn, run in enumerate(runs):
        arriving[turn].wait()
        for tile in range(cut.tiles):
            y = [y_buf[m * cut.tiles + tile, run : run + step].reshape(size, TILE) for m in range(cut.block)]
            lay_out(y, lhs, slice(tile * size, (tile + 1) * size))
        added[turn].wait()
        for pair in pairs:
            for n, piece in exchange_lanes(cut, step, lhs, shuffle, pair):
                for tile in range(cut.tiles):
                    for block in range(step):
                        frame, at = (run + block) * cut.block + n, slice(tile * TILE, (tile + 1) * TILE)
                        x_buf[frame, :, at] = (x_buf[frame, :, at].astype(F32) + piece[tile, block]).astype(BF16)
        leaving += load([(x_buf.at[frames[turn]], out_ref.at[frames[turn], :, lanes])], sems, 2 * RUNS + turn)
    wait_all(leaving)


def filter_kernel(cut, x_ref, spectrum_ref, analysis_h, analysis_l, synthesis_h, synthesis_l, rows_ref, *refs):
    out_ref, x_buf, temporal, wide, column, spectrum, *tables, row_table, shuffle, sems = refs
    every = cut.height * cut.row_blocks
    frame_blocks = cut.tm * cut.frame_blocks
    arriving = load([(x_ref, x_buf), (spectrum_ref, spectrum)], sems)
    arriving += load(zip((analysis_h, analysis_l, synthesis_h, synthesis_l), tables), sems, 2)
    (rows_table,) = load([(rows_ref, row_table)], sems, 2 + len(tables))
    fill_shuffle(cut, shuffle)
    wait_all(arriving)

    def block_rows(n):
        return pl.ds(n, frame_blocks, stride=cut.rows)

    def block_frames(n):
        return pl.ds(n, frame_blocks, stride=cut.block)

    def along_time(j, _):
        for i in range(cut.tm):
            piece = x_buf[i * cut.height + j].astype(F32).reshape(-1, TILE)
            wide[i * piece.shape[0] : (i + 1) * piece.shape[0], :] = piece
        parts = [
            jnp.concatenate(
                [wide[block_rows(block * cut.block + n), :].astype(BF16) for block in range(cut.row_blocks)], axis=0
            )
            for n in range(cut.block)
        ]
        moved = shuffled(parts, shuffle)
        for block in range(cut.row_blocks):
            for n in range(cut.block):
                column[block, block_frames(n), :] = moved[n][block * frame_blocks : (block + 1) * frame_blocks]
        for block in range(0, cut.row_blocks, 2):
            signal = jnp.concatenate([column[block].astype(BF16), column[block + 1].astype(BF16)], axis=1)
            at = pl.ds(pl.multiple_of((j * cut.row_blocks + block) * TILE, WIDE), WIDE)
            temporal[:, at] = filtered(signal, spectrum[...], tables).astype(BF16)
        return _

    def along_rows(j, _):
        for block in range(0, cut.row_blocks, 2):
            first = pairs - 1 - (j * cut.row_blocks + block) // 2
            matrix = row_table[pl.ds(pl.multiple_of(first * WIDE, WIDE), pairs * WIDE), :]
            result = jnp.dot(temporal[...], matrix, preferred_element_type=F32)
            column[block], column[block + 1] = result[:, :TILE], result[:, TILE:]
        parts = [
            jnp.concatenate([column[block, block_frames(n), :].astype(BF16) for block in range(cut.row_blocks)], axis=0)
            for n in range(cut.block)
        ]
        moved = shuffled(parts, shuffle)
        for block in range(cut.row_blocks):
            for n in range(cut.block):
                rows = moved[n][block * frame_blocks : (block + 1) * frame_blocks]
                wide[block_rows(block * cut.block + n), :] = rows
        for i in range(cut.tm):
            count = cut.frame_blocks * cut.rows
            x_buf[i * cut.height + j] = wide[i * count : (i + 1) * count, :].astype(BF16).reshape(cut.piece)
        return _

    pairs = every // 2
    lax.fori_loop(0, cut.height, along_time, 0)
    rows_table.wait()
    lax.fori_loop(0, cut.height, along_rows, 0)
    wait_all(load([(x_buf, out_ref)], sems))


def row_matrices(cut, taps):
    size, own = taps.shape
    near = WIDE // own
    pairs = size // near
    far = np.arange(2 * pairs - 1)[:, None, None]
    source, target = np.arange(near)[None, :, None], np.arange(near)[None, None, :]
    index = ((2 * pairs - 1 - far - pairs) * near + target - source) % size
    chosen = (index.reshape(-1, 1) == np.arange(size)[None, :]).astype(jnp.bfloat16)
    picked = jnp.dot(chosen, taps, preferred_element_type=F32).astype(BF16)
    picked = picked.reshape((2 * pairs - 1) * near, 1, WIDE)
    same = jnp.asarray(np.tile(np.eye(own), (1, near)).astype(jnp.bfloat16))
    return (picked * same[None]).reshape((2 * pairs - 1) * WIDE, WIDE)


def shards(frames_in, time_taps, row_taps):
    frames, rows, lanes = frames_in.shape
    tm, height = lax.axis_size("tm"), lax.axis_size("height")
    if not Cut.fits(frames, rows, lanes, time_taps.shape[1], tm, height):
        return narrow_shards(frames_in, time_taps, row_taps)
    width = lanes // PARTS
    cut = Cut(frames, rows, width, tm, height)
    size = frames * tm
    tables = fourier_tables(size)
    device = lax.axis_index("tm") * height + lax.axis_index("height")

    def free(*arrays):
        return [(array, ANYWHERE) for array in arrays]

    shape = (cut.devices,) + cut.piece
    sems = pltpu.SemaphoreType.DMA((RUNS * (cut.block // 2 + 2) + 8,))
    part_buf, table_buf = pltpu.VMEM((frames, rows, width), BF16), pltpu.VMEM((cut.block * TILE // FOLDS,) * 2, BF16)
    piece_buf = pltpu.VMEM(shape, BF16)
    lhs = pltpu.VMEM((FOLDS, cut.tiles * in_turn(cut)[0] * rows, cut.block * TILE // FOLDS), BF16)

    def exchange(pieces):
        flat = pieces.reshape(cut.devices, -1, TILE)
        return lax.all_to_all(flat, ("tm", "height"), 0, 0, tiled=True).reshape(shape)

    def pack(part):
        kernel = functools.partial(pack_kernel, part * width, cut)
        scratch = [part_buf, table_buf, lhs, piece_buf, sems]
        return exchange(call(kernel, free(frames_in), free(shape), scratch)[0])

    def own_lanes(taps, part):
        first = (part * width + device % cut.tiles * TILE + device // cut.tiles * cut.own) % taps.shape[1]
        return lax.dynamic_slice_in_dim(taps, first, cut.own, axis=1)

    def both(pieces, part):
        taps = jnp.tile(own_lanes(time_taps, part), (1, TILE // cut.own))
        out = ((3, size // 2, TILE), pl.BlockSpec((3, size // 2, TILE), lambda n: (0, 0, 0)))
        (spectrum,) = call(spectrum_kernel, [whole(t) for t in (taps, *tables[:2])], [out], dtype=F32, vmem=FILTER_VMEM)
        matrices = row_matrices(cut, own_lanes(row_taps, part))
        every = rows * height * cut.own
        scratch = [piece_buf, pltpu.VMEM((size, every), BF16), pltpu.VMEM((size // cut.block * rows, TILE), F32)]
        scratch += [pltpu.VMEM((cut.row_blocks, size, TILE), F32), pltpu.VMEM(spectrum.shape, F32)]
        scratch += [pltpu.VMEM(t.shape, BF16) for t in (*tables, matrices)] + [table_buf, sems]
        ins = free(pieces, spectrum, *tables, matrices)
        flops = 2 * size * every * (5 * size + every)
        return exchange(call(functools.partial(filter_kernel, cut), ins, free(shape), scratch, flops, vmem=FILTER_VMEM)[0])

    def unpack_add(pieces, part, held):
        kernel = functools.partial(unpack_add_kernel, part * width, cut)
        scratch = [piece_buf, part_buf, table_buf, lhs, sems]
        return call(kernel, free(pieces, frames_in), free(frames_in.shape), scratch, held=held)[0]

    arrived = [pack(part) for part in range(PARTS)]
    returned = [both(pieces, part) for part, pieces in enumerate(arrived)]
    out = None
    for part, pieces in enumerate(returned):
        out = unpack_add(pieces, part, out)
    return out


def lane_taps(tap_table, first_lane, lane_count):
    channels = tap_table.shape[1]
    distinct = min(lane_count, channels)
    lane_ids = (first_lane + lax.iota(jnp.int32, distinct)) % channels
    selector = (lane_ids[None, :] == lax.iota(jnp.int32, channels)[:, None]).astype(tap_table.dtype)
    picked = jnp.dot(tap_table, selector, preferred_element_type=jnp.float32).astype(
        tap_table.dtype
    )
    return jnp.transpose(picked)


def shifted_taps(taps, base, size):
    distinct, period = taps.shape
    start = (base - (size - 1)) % period
    tiled = jnp.concatenate([taps, taps, taps], axis=1)
    window = lax.slice_in_dim(tiled, start, start + 2 * size - 1, axis=1)
    reversed_window = window[:, ::-1]
    padded = jnp.concatenate([reversed_window, jnp.zeros((distinct, 1), taps.dtype)], axis=1)
    repeated = jnp.tile(padded, (1, size + 1))
    flat = lax.slice_in_dim(repeated, size - 1, size - 1 + size * (2 * size - 1), axis=1)
    return flat.reshape(distinct, size, 2 * size - 1)[:, :, :size]


def time_convolve(segment, own_taps):
    frames, rows_here, lane_count = segment.shape
    distinct = own_taps.shape[0]
    columns = lane_count // distinct
    block_len = min(128, frames)
    block_count = frames // block_len
    blocked = segment.reshape(block_count, block_len, rows_here, columns, distinct)
    blocked = jnp.transpose(blocked, (4, 3, 2, 0, 1))
    running = jnp.zeros((distinct, columns, rows_here, block_count, block_len), jnp.float32)
    for lag_index in range(block_count):
        toeplitz = shifted_taps(own_taps, lag_index * block_len, block_len)
        rolled = jnp.roll(blocked, lag_index, axis=3)
        running = running + jnp.einsum(
            "cab,cxrnb->cxrna", toeplitz, rolled, preferred_element_type=jnp.float32
        )
    result = jnp.transpose(running, (3, 4, 2, 1, 0)).reshape(frames, rows_here, lane_count)
    return result.astype(jnp.bfloat16)


def row_convolve(segment, row_taps):
    frames, height, lane_count = segment.shape
    distinct = row_taps.shape[0]
    columns = lane_count // distinct
    arranged = jnp.transpose(segment.reshape(frames, height, columns, distinct), (3, 2, 0, 1))
    circulant = shifted_taps(row_taps, 0, height)
    filtered = jnp.einsum("cab,cxfb->cxfa", circulant, arranged, preferred_element_type=jnp.float32)
    result = jnp.transpose(filtered, (2, 3, 1, 0)).reshape(frames, height, lane_count)
    return result.astype(jnp.bfloat16)


def narrow_shards(frames_in, time_filter, height_filter):
    frames_dev, rows_dev, lane_total = frames_in.shape
    tm_count = lax.axis_size("tm")
    height_count = lax.axis_size("height")
    lane_count = lane_total // (tm_count * height_count)
    first_lane = (
        lax.axis_index("tm") * (lane_total // tm_count) + lax.axis_index("height") * lane_count
    )
    own_taps = lane_taps(time_filter, first_lane, lane_count)
    row_taps = lane_taps(height_filter, first_lane, lane_count)
    gathered = lax.all_to_all(
        lax.all_to_all(frames_in, "tm", split_axis=2, concat_axis=0, tiled=True),
        "height",
        split_axis=2,
        concat_axis=1,
        tiled=True,
    )
    temporal = time_convolve(gathered, own_taps)
    spatial_lanes = row_convolve(temporal, row_taps)
    returned = lax.all_to_all(
        lax.all_to_all(spatial_lanes, "tm", split_axis=0, concat_axis=2, tiled=True),
        "height",
        split_axis=1,
        concat_axis=2,
        tiled=True,
    )
    spatial = returned.reshape(frames_dev, rows_dev, height_count, tm_count, lane_count)
    spatial = jnp.transpose(spatial, (0, 1, 3, 2, 4)).reshape(frames_dev, rows_dev, lane_total)
    return (frames_in.astype(jnp.float32) + spatial.astype(jnp.float32)).astype(jnp.bfloat16)


def solution(mesh):
    return jax.shard_map(
        shards,
        mesh=mesh,
        in_specs=(P("tm", "height", None), P(), P()),
        out_specs=P("tm", "height", None),
        check_vma=False,
    )
```

```python
import functools

import jax
import jax.numpy as jnp
import numpy as np
from jax import lax
from jax.experimental import pallas as pl
from jax.experimental.pallas import tpu as pltpu
from jax.sharding import PartitionSpec as P

F32, BF16 = jnp.float32, jnp.bfloat16
TILE = 128
WIDE = 2 * TILE
PARTS = 2
RUNS = 2
FOLDS = 2
VMEM_BYTES = 62 << 20
FILTER_VMEM = 40 << 20
ANYWHERE = pl.BlockSpec(memory_space=pl.ANY)


def split_terms(table):
    high = table.astype(jnp.bfloat16)
    low = (table - high.astype(np.float64)).astype(jnp.bfloat16)
    return high, low


def fourier_tables(size):
    half = size // 2
    wave, at = np.arange(half)[:, None], np.arange(size)[None, :]
    angle = 2.0 * np.pi * ((wave * at) % size) / size
    sines = np.sin(angle)
    sines[0] = 1.0 - 2.0 * (np.arange(size) % 2)
    analysis = np.concatenate([np.cos(angle), sines], axis=0)
    weight = np.full((size,), 2.0 / size)
    weight[0] = weight[half] = 1.0 / size
    synthesis = (analysis * weight[:, None]).T
    return split_terms(analysis) + split_terms(synthesis)


def spectrum_kernel(taps_ref, high_ref, low_ref, out_ref):
    half = taps_ref.shape[0] // 2
    sums = jnp.dot(high_ref[...], taps_ref[...], preferred_element_type=F32)
    sums += jnp.dot(low_ref[...], taps_ref[...], preferred_element_type=F32)
    cosines, sines = sums[:half], sums[half:]
    first = lax.broadcasted_iota(jnp.int32, cosines.shape, 0) == 0
    out_ref[0] = cosines
    out_ref[1] = jnp.where(first, 0.0, sines)
    out_ref[2] = jnp.where(first, sines, cosines)


def filtered(signal, spectrum, tables):
    half = spectrum.shape[1]
    analysis_high, analysis_low, synthesis_high, synthesis_low = (t[...] for t in tables)
    coef = jnp.dot(analysis_high, signal, preferred_element_type=F32)
    coef += jnp.dot(analysis_low, signal, preferred_element_type=F32)
    cos_part, sin_part = coef[:half], coef[half:]
    keep, turn, other = (jnp.concatenate([spectrum[n]] * (signal.shape[1] // TILE), axis=1) for n in range(3))
    product = jnp.concatenate([cos_part * keep - sin_part * turn, sin_part * other + cos_part * turn], axis=0)
    high = product.astype(BF16)
    low = (product - high.astype(F32)).astype(BF16)
    result = jnp.dot(synthesis_high, high, preferred_element_type=F32)
    result += jnp.dot(synthesis_low, high, preferred_element_type=F32)
    result += jnp.dot(synthesis_high, low, preferred_element_type=F32)
    return result


class Cut:
    def __init__(self, frames, rows, width, tm, height):
        self.frames, self.rows, self.width, self.tm, self.height = frames, rows, width, tm, height
        self.devices = tm * height
        self.own = width // self.devices
        self.block = TILE // self.own
        self.frame_blocks, self.row_blocks = frames // self.block, rows // self.block
        self.tiles = width // TILE
        self.piece = (self.frame_blocks, rows, TILE)

    @staticmethod
    def fits(frames, rows, lanes, channels, tm, height):
        own = lanes // PARTS // (tm * height)
        if own == 0 or TILE % own or lanes != PARTS * own * tm * height or lanes // PARTS % TILE or channels % own:
            return False
        block = TILE // own
        return frames % block == 0 and rows % block == 0 and rows % 16 == 0 and rows // block % 2 == 0 and block % (2 * FOLDS) == 0


def call(kernel, ins, outs, scratch=(), flops=0, held=None, dtype=BF16, vmem=VMEM_BYTES):
    unread = [] if held is None else [held]

    def body(*refs):
        kernel(*refs[: len(ins)], *refs[len(ins) + len(unread) :])

    moved = 2 * sum(int(np.prod(a.shape)) for a, _ in ins) + 2 * sum(int(np.prod(s)) for s, _ in outs)
    return pl.pallas_call(
        body,
        grid=(1,),
        in_specs=[spec for _, spec in ins] + [ANYWHERE] * len(unread),
        out_specs=[spec for _, spec in outs],
        out_shape=[jax.ShapeDtypeStruct(shape, dtype) for shape, _ in outs],
        scratch_shapes=list(scratch),
        input_output_aliases={} if held is None else {len(ins): 0},
        compiler_params=pltpu.CompilerParams(vmem_limit_bytes=vmem),
        cost_estimate=pl.CostEstimate(flops=flops, bytes_accessed=moved, transcendentals=0),
    )(*[array for array, _ in ins], *unread)


def whole(table):
    return table, pl.BlockSpec(table.shape, lambda n: (0,) * table.ndim)


def start_all(copies):
    for copy in copies:
        copy.start()
    return copies


def wait_all(copies):
    for copy in copies:
        copy.wait()


def load(pairs, sems, first=0):
    return start_all([pltpu.make_async_copy(a, b, sems.at[first + n]) for n, (a, b) in enumerate(pairs)])


def fill_shuffle(cut, shuffle):
    row = lax.broadcasted_iota(jnp.int32, shuffle.shape, 0)
    column = lax.broadcasted_iota(jnp.int32, (1, shuffle.shape[1]), 1)
    m, n, lane = column // TILE, column % TILE // cut.own, column % cut.own
    shuffle[...] = (row == n * (TILE // FOLDS) + m * cut.own + lane).astype(F32).astype(BF16)


def folds(tiles):
    for fold in range(FOLDS):
        lanes = slice(fold * TILE // FOLDS, (fold + 1) * TILE // FOLDS)
        yield [
            jnp.concatenate([tile[:, lanes] for tile in tiles[n : n + FOLDS]], axis=1)
            for n in range(0, len(tiles), FOLDS)
        ]


def shuffled(tiles, shuffle):
    result = []
    for part in folds(tiles):
        moved = jnp.dot(jnp.concatenate(part, axis=1), shuffle[...], preferred_element_type=F32)
        result += [moved[:, m * TILE : (m + 1) * TILE] for m in range(len(tiles) // FOLDS)]
    return result


def lay_out(tiles, lhs, rows):
    for fold, part in enumerate(folds(tiles)):
        for n, tile in enumerate(part):
            lhs[fold, rows, n * TILE : (n + 1) * TILE] = tile


def in_turn(cut):
    count = next(n for n in (RUNS, 1) if cut.frame_blocks % n == 0)
    step = cut.frame_blocks // count
    return step, range(0, cut.frame_blocks, step), range(0, cut.block, 2)


def exchange_lanes(cut, step, lhs, shuffle, first):
    fold, at = divmod(first, cut.block // FOLDS)
    moved = jnp.dot(lhs[fold], shuffle[:, at * TILE : (at + 2) * TILE], preferred_element_type=F32)
    shape = (cut.tiles, step, cut.rows, TILE)
    return [(first + n, moved[:, n * TILE : (n + 1) * TILE].reshape(shape)) for n in range(2)]


def pack_kernel(lane, cut, x_ref, out_ref, x_buf, shuffle, lhs, out_buf, sems):
    step, runs, pairs = in_turn(cut)
    size = step * cut.rows
    frames = [pl.ds(run * cut.block, step * cut.block) for run in runs]
    arriving = load([(x_ref.at[at, :, pl.ds(lane, cut.width)], x_buf.at[at]) for at in frames], sems)
    fill_shuffle(cut, shuffle)
    leaving = []
    for turn, run in enumerate(runs):
        arriving[turn].wait()
        for tile in range(cut.tiles):
            lanes = slice(tile * TILE, (tile + 1) * TILE)
            x = x_buf[frames[turn], :, lanes].reshape(step, cut.block, cut.rows, TILE)
            lay_out([x[:, n].reshape(size, TILE) for n in range(cut.block)], lhs, slice(tile * size, (tile + 1) * size))
        for pair in pairs:
            for m, piece in exchange_lanes(cut, step, lhs, shuffle, pair):
                for tile in range(cut.tiles):
                    out_buf[m * cut.tiles + tile, run : run + step] = piece[tile].astype(BF16)
            some = (pl.ds(pair * cut.tiles, 2 * cut.tiles), pl.ds(run, step))
            leaving += load([(out_buf.at[some], out_ref.at[some])], sems, len(runs) + len(leaving))
    wait_all(leaving)


def unpack_add_kernel(lane, cut, y_ref, x_ref, out_ref, y_buf, x_buf, shuffle, lhs, sems):
    step, runs, pairs = in_turn(cut)
    size = step * cut.rows
    lanes = pl.ds(lane, cut.width)
    parts = [pl.ds(run, step) for run in runs]
    frames = [pl.ds(run * cut.block, step * cut.block) for run in runs]
    arriving, added = [], []
    for turn, (part, at) in enumerate(zip(parts, frames)):
        arriving += load([(y_ref.at[:, part], y_buf.at[:, part])], sems, turn)
        added += load([(x_ref.at[at, :, lanes], x_buf.at[at])], sems, RUNS + turn)
    fill_shuffle(cut, shuffle)
    leaving = []
    for turn, run in enumerate(runs):
        arriving[turn].wait()
        for tile in range(cut.tiles):
            y = [y_buf[m * cut.tiles + tile, run : run + step].reshape(size, TILE) for m in range(cut.block)]
            lay_out(y, lhs, slice(tile * size, (tile + 1) * size))
        added[turn].wait()
        for pair in pairs:
            for n, piece in exchange_lanes(cut, step, lhs, shuffle, pair):
                for tile in range(cut.tiles):
                    for block in range(step):
                        frame, at = (run + block) * cut.block + n, slice(tile * TILE, (tile + 1) * TILE)
                        x_buf[frame, :, at] = (x_buf[frame, :, at].astype(F32) + piece[tile, block]).astype(BF16)
        leaving += load([(x_buf.at[frames[turn]], out_ref.at[frames[turn], :, lanes])], sems, 2 * RUNS + turn)
    wait_all(leaving)


def filter_kernel(cut, x_ref, spectrum_ref, analysis_h, analysis_l, synthesis_h, synthesis_l, rows_ref, *refs):
    out_ref, x_buf, temporal, wide, column, spectrum, *tables, row_table, shuffle, sems = refs
    every = cut.height * cut.row_blocks
    frame_blocks = cut.tm * cut.frame_blocks
    arriving = load([(x_ref, x_buf), (spectrum_ref, spectrum)], sems)
    arriving += load(zip((analysis_h, analysis_l, synthesis_h, synthesis_l), tables), sems, 2)
    (rows_table,) = load([(rows_ref, row_table)], sems, 2 + len(tables))
    fill_shuffle(cut, shuffle)
    wait_all(arriving)

    def block_rows(n):
        return pl.ds(n, frame_blocks, stride=cut.rows)

    def block_frames(n):
        return pl.ds(n, frame_blocks, stride=cut.block)

    def along_time(j, _):
        for i in range(cut.tm):
            piece = x_buf[i * cut.height + j].astype(F32).reshape(-1, TILE)
            wide[i * piece.shape[0] : (i + 1) * piece.shape[0], :] = piece
        parts = [
            jnp.concatenate(
                [wide[block_rows(block * cut.block + n), :].astype(BF16) for block in range(cut.row_blocks)], axis=0
            )
            for n in range(cut.block)
        ]
        moved = shuffled(parts, shuffle)
        for block in range(cut.row_blocks):
            for n in range(cut.block):
                column[block, block_frames(n), :] = moved[n][block * frame_blocks : (block + 1) * frame_blocks]
        for block in range(0, cut.row_blocks, 2):
            signal = jnp.concatenate([column[block].astype(BF16), column[block + 1].astype(BF16)], axis=1)
            at = pl.ds(pl.multiple_of((j * cut.row_blocks + block) * TILE, WIDE), WIDE)
            temporal[:, at] = filtered(signal, spectrum[...], tables).astype(BF16)
        return _

    def along_rows(j, _):
        for block in range(0, cut.row_blocks, 2):
            first = pairs - 1 - (j * cut.row_blocks + block) // 2
            matrix = row_table[pl.ds(pl.multiple_of(first * WIDE, WIDE), pairs * WIDE), :]
            result = jnp.dot(temporal[...], matrix, preferred_element_type=F32)
            column[block], column[block + 1] = result[:, :TILE], result[:, TILE:]
        parts = [
            jnp.concatenate([column[block, block_frames(n), :].astype(BF16) for block in range(cut.row_blocks)], axis=0)
            for n in range(cut.block)
        ]
        moved = shuffled(parts, shuffle)
        for block in range(cut.row_blocks):
            for n in range(cut.block):
                rows = moved[n][block * frame_blocks : (block + 1) * frame_blocks]
                wide[block_rows(block * cut.block + n), :] = rows
        for i in range(cut.tm):
            count = cut.frame_blocks * cut.rows
            x_buf[i * cut.height + j] = wide[i * count : (i + 1) * count, :].astype(BF16).reshape(cut.piece)
        return _

    pairs = every // 2
    lax.fori_loop(0, cut.height, along_time, 0)
    rows_table.wait()
    lax.fori_loop(0, cut.height, along_rows, 0)
    wait_all(load([(x_buf, out_ref)], sems))


def row_matrices(cut, taps):
    size, own = taps.shape
    near = WIDE // own
    pairs = size // near
    far = np.arange(2 * pairs - 1)[:, None, None]
    source, target = np.arange(near)[None, :, None], np.arange(near)[None, None, :]
    index = ((2 * pairs - 1 - far - pairs) * near + target - source) % size
    chosen = (index.reshape(-1, 1) == np.arange(size)[None, :]).astype(jnp.bfloat16)
    picked = jnp.dot(chosen, taps, preferred_element_type=F32).astype(BF16)
    picked = picked.reshape((2 * pairs - 1) * near, 1, WIDE)
    same = jnp.asarray(np.tile(np.eye(own), (1, near)).astype(jnp.bfloat16))
    return (picked * same[None]).reshape((2 * pairs - 1) * WIDE, WIDE)


def shards(frames_in, time_taps, row_taps):
    frames, rows, lanes = frames_in.shape
    tm, height = lax.axis_size("tm"), lax.axis_size("height")
    if not Cut.fits(frames, rows, lanes, time_taps.shape[1], tm, height):
        return narrow_shards(frames_in, time_taps, row_taps)
    width = lanes // PARTS
    cut = Cut(frames, rows, width, tm, height)
    size = frames * tm
    tables = fourier_tables(size)
    device = lax.axis_index("tm") * height + lax.axis_index("height")

    def free(*arrays):
        return [(array, ANYWHERE) for array in arrays]

    shape = (cut.devices,) + cut.piece
    sems = pltpu.SemaphoreType.DMA((RUNS * (cut.block // 2 + 2) + 8,))
    part_buf, table_buf = pltpu.VMEM((frames, rows, width), BF16), pltpu.VMEM((cut.block * TILE // FOLDS,) * 2, BF16)
    piece_buf = pltpu.VMEM(shape, BF16)
    lhs = pltpu.VMEM((FOLDS, cut.tiles * in_turn(cut)[0] * rows, cut.block * TILE // FOLDS), BF16)

    def exchange(pieces):
        flat = pieces.reshape(cut.devices, -1, TILE)
        return lax.all_to_all(flat, ("tm", "height"), 0, 0, tiled=True).reshape(shape)

    def pack(part):
        kernel = functools.partial(pack_kernel, part * width, cut)
        scratch = [part_buf, table_buf, lhs, piece_buf, sems]
        return exchange(call(kernel, free(frames_in), free(shape), scratch)[0])

    def own_lanes(taps, part):
        first = (part * width + device % cut.tiles * TILE + device // cut.tiles * cut.own) % taps.shape[1]
        return lax.dynamic_slice_in_dim(taps, first, cut.own, axis=1)

    def both(pieces, part):
        taps = jnp.tile(own_lanes(time_taps, part), (1, TILE // cut.own))
        out = ((3, size // 2, TILE), pl.BlockSpec((3, size // 2, TILE), lambda n: (0, 0, 0)))
        (spectrum,) = call(spectrum_kernel, [whole(t) for t in (taps, *tables[:2])], [out], dtype=F32, vmem=FILTER_VMEM)
        matrices = row_matrices(cut, own_lanes(row_taps, part))
        every = rows * height * cut.own
        scratch = [piece_buf, pltpu.VMEM((size, every), BF16), pltpu.VMEM((size // cut.block * rows, TILE), F32)]
        scratch += [pltpu.VMEM((cut.row_blocks, size, TILE), F32), pltpu.VMEM(spectrum.shape, F32)]
        scratch += [pltpu.VMEM(t.shape, BF16) for t in (*tables, matrices)] + [table_buf, sems]
        ins = free(pieces, spectrum, *tables, matrices)
        flops = 2 * size * every * (5 * size + every)
        return exchange(call(functools.partial(filter_kernel, cut), ins, free(shape), scratch, flops, vmem=FILTER_VMEM)[0])

    def unpack_add(pieces, part, held):
        kernel = functools.partial(unpack_add_kernel, part * width, cut)
        scratch = [piece_buf, part_buf, table_buf, lhs, sems]
        return call(kernel, free(pieces, frames_in), free(frames_in.shape), scratch, held=held)[0]

    arrived = [pack(part) for part in range(PARTS)]
    returned = [both(pieces, part) for part, pieces in enumerate(arrived)]
    out = None
    for part, pieces in enumerate(returned):
        out = unpack_add(pieces, part, out)
    return out


def lane_taps(tap_table, first_lane, lane_count):
    channels = tap_table.shape[1]
    distinct = min(lane_count, channels)
    lane_ids = (first_lane + lax.iota(jnp.int32, distinct)) % channels
    selector = (lane_ids[None, :] == lax.iota(jnp.int32, channels)[:, None]).astype(tap_table.dtype)
    picked = jnp.dot(tap_table, selector, preferred_element_type=jnp.float32).astype(
        tap_table.dtype
    )
    return jnp.transpose(picked)


def shifted_taps(taps, base, size):
    distinct, period = taps.shape
    start = (base - (size - 1)) % period
    tiled = jnp.concatenate([taps, taps, taps], axis=1)
    window = lax.slice_in_dim(tiled, start, start + 2 * size - 1, axis=1)
    reversed_window = window[:, ::-1]
    padded = jnp.concatenate([reversed_window, jnp.zeros((distinct, 1), taps.dtype)], axis=1)
    repeated = jnp.tile(padded, (1, size + 1))
    flat = lax.slice_in_dim(repeated, size - 1, size - 1 + size * (2 * size - 1), axis=1)
    return flat.reshape(distinct, size, 2 * size - 1)[:, :, :size]


def time_convolve(segment, own_taps):
    frames, rows_here, lane_count = segment.shape
    distinct = own_taps.shape[0]
    columns = lane_count // distinct
    block_len = min(128, frames)
    block_count = frames // block_len
    blocked = segment.reshape(block_count, block_len, rows_here, columns, distinct)
    blocked = jnp.transpose(blocked, (4, 3, 2, 0, 1))
    running = jnp.zeros((distinct, columns, rows_here, block_count, block_len), jnp.float32)
    for lag_index in range(block_count):
        toeplitz = shifted_taps(own_taps, lag_index * block_len, block_len)
        rolled = jnp.roll(blocked, lag_index, axis=3)
        running = running + jnp.einsum(
            "cab,cxrnb->cxrna", toeplitz, rolled, preferred_element_type=jnp.float32
        )
    result = jnp.transpose(running, (3, 4, 2, 1, 0)).reshape(frames, rows_here, lane_count)
    return result.astype(jnp.bfloat16)


def row_convolve(segment, row_taps):
    frames, height, lane_count = segment.shape
    distinct = row_taps.shape[0]
    columns = lane_count // distinct
    arranged = jnp.transpose(segment.reshape(frames, height, columns, distinct), (3, 2, 0, 1))
    circulant = shifted_taps(row_taps, 0, height)
    filtered = jnp.einsum("cab,cxfb->cxfa", circulant, arranged, preferred_element_type=jnp.float32)
    result = jnp.transpose(filtered, (2, 3, 1, 0)).reshape(frames, height, lane_count)
    return result.astype(jnp.bfloat16)


def narrow_shards(frames_in, time_filter, height_filter):
    frames_dev, rows_dev, lane_total = frames_in.shape
    tm_count = lax.axis_size("tm")
    height_count = lax.axis_size("height")
    lane_count = lane_total // (tm_count * height_count)
    first_lane = (
        lax.axis_index("tm") * (lane_total // tm_count) + lax.axis_index("height") * lane_count
    )
    own_taps = lane_taps(time_filter, first_lane, lane_count)
    row_taps = lane_taps(height_filter, first_lane, lane_count)
    gathered = lax.all_to_all(
        lax.all_to_all(frames_in, "tm", split_axis=2, concat_axis=0, tiled=True),
        "height",
        split_axis=2,
        concat_axis=1,
        tiled=True,
    )
    temporal = time_convolve(gathered, own_taps)
    spatial_lanes = row_convolve(temporal, row_taps)
    returned = lax.all_to_all(
        lax.all_to_all(spatial_lanes, "tm", split_axis=0, concat_axis=2, tiled=True),
        "height",
        split_axis=1,
        concat_axis=2,
        tiled=True,
    )
    spatial = returned.reshape(frames_dev, rows_dev, height_count, tm_count, lane_count)
    spatial = jnp.transpose(spatial, (0, 1, 3, 2, 4)).reshape(frames_dev, rows_dev, lane_total)
    return (frames_in.astype(jnp.float32) + spatial.astype(jnp.float32)).astype(jnp.bfloat16)


def solution(mesh):
    return jax.shard_map(
        shards,
        mesh=mesh,
        in_specs=(P("tm", "height", None), P(), P()),
        out_specs=P("tm", "height", None),
        check_vma=False,
    )
```

```python
import functools

import jax
import jax.numpy as jnp
import numpy as np
from jax import lax
from jax.experimental import pallas as pl
from jax.experimental.pallas import tpu as pltpu
from jax.sharding import PartitionSpec as P

F32, BF16 = jnp.float32, jnp.bfloat16
TILE = 128
WIDE = 2 * TILE
PARTS = 2
RUNS = 2
FOLDS = 2
VMEM_BYTES = 62 << 20
FILTER_VMEM = 40 << 20
ANYWHERE = pl.BlockSpec(memory_space=pl.ANY)


def split_terms(table):
    high = table.astype(jnp.bfloat16)
    low = (table - high.astype(np.float64)).astype(jnp.bfloat16)
    return high, low


def fourier_tables(size):
    half = size // 2
    wave, at = np.arange(half)[:, None], np.arange(size)[None, :]
    angle = 2.0 * np.pi * ((wave * at) % size) / size
    sines = np.sin(angle)
    sines[0] = 1.0 - 2.0 * (np.arange(size) % 2)
    analysis = np.concatenate([np.cos(angle), sines], axis=0)
    weight = np.full((size,), 2.0 / size)
    weight[0] = weight[half] = 1.0 / size
    synthesis = (analysis * weight[:, None]).T
    return split_terms(analysis) + split_terms(synthesis)


def spectrum_kernel(taps_ref, high_ref, low_ref, out_ref):
    half = taps_ref.shape[0] // 2
    sums = jnp.dot(high_ref[...], taps_ref[...], preferred_element_type=F32)
    sums += jnp.dot(low_ref[...], taps_ref[...], preferred_element_type=F32)
    cosines, sines = sums[:half], sums[half:]
    first = lax.broadcasted_iota(jnp.int32, cosines.shape, 0) == 0
    out_ref[0] = cosines
    out_ref[1] = jnp.where(first, 0.0, sines)
    out_ref[2] = jnp.where(first, sines, cosines)


def filtered(signal, spectrum, tables):
    half = spectrum.shape[1]
    analysis_high, analysis_low, synthesis_high, synthesis_low = (t[...] for t in tables)
    coef = jnp.dot(analysis_high, signal, preferred_element_type=F32)
    coef += jnp.dot(analysis_low, signal, preferred_element_type=F32)
    cos_part, sin_part = coef[:half], coef[half:]
    keep, turn, other = (jnp.concatenate([spectrum[n]] * (signal.shape[1] // TILE), axis=1) for n in range(3))
    product = jnp.concatenate([cos_part * keep - sin_part * turn, sin_part * other + cos_part * turn], axis=0)
    high = product.astype(BF16)
    low = (product - high.astype(F32)).astype(BF16)
    result = jnp.dot(synthesis_high, high, preferred_element_type=F32)
    result += jnp.dot(synthesis_low, high, preferred_element_type=F32)
    result += jnp.dot(synthesis_high, low, preferred_element_type=F32)
    return result


class Cut:
    def __init__(self, frames, rows, width, tm, height):
        self.frames, self.rows, self.width, self.tm, self.height = frames, rows, width, tm, height
        self.devices = tm * height
        self.own = width // self.devices
        self.block = TILE // self.own
        self.frame_blocks, self.row_blocks = frames // self.block, rows // self.block
        self.tiles = width // TILE
        self.piece = (self.frame_blocks, rows, TILE)

    @staticmethod
    def fits(frames, rows, lanes, channels, tm, height):
        own = lanes // PARTS // (tm * height)
        if own == 0 or TILE % own or lanes != PARTS * own * tm * height or lanes // PARTS % TILE or channels % own:
            return False
        block = TILE // own
        return frames % block == 0 and rows % block == 0 and rows % 16 == 0 and rows // block % 2 == 0 and block % (2 * FOLDS) == 0


def call(kernel, ins, outs, scratch=(), flops=0, held=None, dtype=BF16, vmem=VMEM_BYTES):
    unread = [] if held is None else [held]

    def body(*refs):
        kernel(*refs[: len(ins)], *refs[len(ins) + len(unread) :])

    moved = 2 * sum(int(np.prod(a.shape)) for a, _ in ins) + 2 * sum(int(np.prod(s)) for s, _ in outs)
    return pl.pallas_call(
        body,
        grid=(1,),
        in_specs=[spec for _, spec in ins] + [ANYWHERE] * len(unread),
        out_specs=[spec for _, spec in outs],
        out_shape=[jax.ShapeDtypeStruct(shape, dtype) for shape, _ in outs],
        scratch_shapes=list(scratch),
        input_output_aliases={} if held is None else {len(ins): 0},
        compiler_params=pltpu.CompilerParams(vmem_limit_bytes=vmem),
        cost_estimate=pl.CostEstimate(flops=flops, bytes_accessed=moved, transcendentals=0),
    )(*[array for array, _ in ins], *unread)


def whole(table):
    return table, pl.BlockSpec(table.shape, lambda n: (0,) * table.ndim)


def start_all(copies):
    for copy in copies:
        copy.start()
    return copies


def wait_all(copies):
    for copy in copies:
        copy.wait()


def load(pairs, sems, first=0):
    return start_all([pltpu.make_async_copy(a, b, sems.at[first + n]) for n, (a, b) in enumerate(pairs)])


def fill_shuffle(cut, shuffle):
    row = lax.broadcasted_iota(jnp.int32, shuffle.shape, 0)
    column = lax.broadcasted_iota(jnp.int32, (1, shuffle.shape[1]), 1)
    m, n, lane = column // TILE, column % TILE // cut.own, column % cut.own
    shuffle[...] = (row == n * (TILE // FOLDS) + m * cut.own + lane).astype(F32).astype(BF16)


def folds(tiles):
    for fold in range(FOLDS):
        lanes = slice(fold * TILE // FOLDS, (fold + 1) * TILE // FOLDS)
        yield [
            jnp.concatenate([tile[:, lanes] for tile in tiles[n : n + FOLDS]], axis=1)
            for n in range(0, len(tiles), FOLDS)
        ]


def shuffled(tiles, shuffle):
    result = []
    for part in folds(tiles):
        moved = jnp.dot(jnp.concatenate(part, axis=1), shuffle[...], preferred_element_type=F32)
        result += [moved[:, m * TILE : (m + 1) * TILE] for m in range(len(tiles) // FOLDS)]
    return result


def lay_out(tiles, lhs, rows):
    for fold, part in enumerate(folds(tiles)):
        for n, tile in enumerate(part):
            lhs[fold, rows, n * TILE : (n + 1) * TILE] = tile


def in_turn(cut):
    count = next(n for n in (RUNS, 1) if cut.frame_blocks % n == 0)
    step = cut.frame_blocks // count
    return step, range(0, cut.frame_blocks, step), range(0, cut.block, 2)


def exchange_lanes(cut, step, lhs, shuffle, first):
    fold, at = divmod(first, cut.block // FOLDS)
    moved = jnp.dot(lhs[fold], shuffle[:, at * TILE : (at + 2) * TILE], preferred_element_type=F32)
    shape = (cut.tiles, step, cut.rows, TILE)
    return [(first + n, moved[:, n * TILE : (n + 1) * TILE].reshape(shape)) for n in range(2)]


def pack_kernel(lane, cut, x_ref, out_ref, x_buf, shuffle, lhs, out_buf, sems):
    step, runs, pairs = in_turn(cut)
    size = step * cut.rows
    frames = [pl.ds(run * cut.block, step * cut.block) for run in runs]
    arriving = load([(x_ref.at[at, :, pl.ds(lane, cut.width)], x_buf.at[at]) for at in frames], sems)
    fill_shuffle(cut, shuffle)
    leaving = []
    for turn, run in enumerate(runs):
        arriving[turn].wait()
        for tile in range(cut.tiles):
            lanes = slice(tile * TILE, (tile + 1) * TILE)
            x = x_buf[frames[turn], :, lanes].reshape(step, cut.block, cut.rows, TILE)
            lay_out([x[:, n].reshape(size, TILE) for n in range(cut.block)], lhs, slice(tile * size, (tile + 1) * size))
        for pair in pairs:
            for m, piece in exchange_lanes(cut, step, lhs, shuffle, pair):
                for tile in range(cut.tiles):
                    out_buf[m * cut.tiles + tile, run : run + step] = piece[tile].astype(BF16)
            some = (pl.ds(pair * cut.tiles, 2 * cut.tiles), pl.ds(run, step))
            leaving += load([(out_buf.at[some], out_ref.at[some])], sems, len(runs) + len(leaving))
    wait_all(leaving)


def unpack_add_kernel(lane, cut, y_ref, x_ref, out_ref, y_buf, x_buf, shuffle, lhs, sems):
    step, runs, pairs = in_turn(cut)
    size = step * cut.rows
    lanes = pl.ds(lane, cut.width)
    parts = [pl.ds(run, step) for run in runs]
    frames = [pl.ds(run * cut.block, step * cut.block) for run in runs]
    arriving, added = [], []
    for turn, (part, at) in enumerate(zip(parts, frames)):
        arriving += load([(y_ref.at[:, part], y_buf.at[:, part])], sems, turn)
        added += load([(x_ref.at[at, :, lanes], x_buf.at[at])], sems, RUNS + turn)
    fill_shuffle(cut, shuffle)
    leaving = []
    for turn, run in enumerate(runs):
        arriving[turn].wait()
        for tile in range(cut.tiles):
            y = [y_buf[m * cut.tiles + tile, run : run + step].reshape(size, TILE) for m in range(cut.block)]
            lay_out(y, lhs, slice(tile * size, (tile + 1) * size))
        added[turn].wait()
        for pair in pairs:
            for n, piece in exchange_lanes(cut, step, lhs, shuffle, pair):
                for tile in range(cut.tiles):
                    for block in range(step):
                        frame, at = (run + block) * cut.block + n, slice(tile * TILE, (tile + 1) * TILE)
                        x_buf[frame, :, at] = (x_buf[frame, :, at].astype(F32) + piece[tile, block]).astype(BF16)
        leaving += load([(x_buf.at[frames[turn]], out_ref.at[frames[turn], :, lanes])], sems, 2 * RUNS + turn)
    wait_all(leaving)


def filter_kernel(cut, x_ref, spectrum_ref, analysis_h, analysis_l, synthesis_h, synthesis_l, rows_ref, *refs):
    out_ref, x_buf, temporal, wide, column, spectrum, *tables, row_table, shuffle, sems = refs
    every = cut.height * cut.row_blocks
    frame_blocks = cut.tm * cut.frame_blocks
    size = cut.tm * cut.frames
    arriving = load([(x_ref, x_buf), (spectrum_ref, spectrum)], sems)
    arriving += load(zip((analysis_h, analysis_l, synthesis_h, synthesis_l), tables), sems, 2)
    (rows_table,) = load([(rows_ref, row_table)], sems, 2 + len(tables))
    fill_shuffle(cut, shuffle)
    wait_all(arriving)

    def block_rows(n):
        return pl.ds(n, frame_blocks, stride=cut.rows)

    def block_frames(n):
        return pl.ds(n, frame_blocks, stride=cut.block)

    def along_time(j, _):
        for i in range(cut.tm):
            piece = x_buf[i * cut.height + j].astype(F32).reshape(-1, TILE)
            wide[i * piece.shape[0] : (i + 1) * piece.shape[0], :] = piece
        parts = [
            jnp.concatenate(
                [wide[block_rows(block * cut.block + n), :].astype(BF16) for block in range(cut.row_blocks)], axis=0
            )
            for n in range(cut.block)
        ]
        moved = shuffled(parts, shuffle)
        for block in range(cut.row_blocks):
            for n in range(cut.block):
                column[block, block_frames(n), :] = moved[n][block * frame_blocks : (block + 1) * frame_blocks]
        for block in range(0, cut.row_blocks, 2):
            signal = jnp.concatenate([column[block + n, :size].astype(BF16) for n in range(2)], axis=1)
            at = pl.ds(pl.multiple_of((j * cut.row_blocks + block) * TILE, WIDE), WIDE)
            temporal[:, at] = filtered(signal, spectrum[...], tables).astype(BF16)
        return _

    def along_rows(j, _):
        for block in range(0, cut.row_blocks, 2):
            first = pairs - 1 - (j * cut.row_blocks + block) // 2
            matrix = row_table[pl.ds(pl.multiple_of(first * WIDE, WIDE), pairs * WIDE), :]
            result = jnp.dot(temporal[...], matrix, preferred_element_type=F32)
            column[block, :size], column[block + 1, :size] = result[:, :TILE], result[:, TILE:]
        parts = [
            jnp.concatenate([column[block, block_frames(n), :].astype(BF16) for block in range(cut.row_blocks)], axis=0)
            for n in range(cut.block)
        ]
        moved = shuffled(parts, shuffle)
        for block in range(cut.row_blocks):
            for n in range(cut.block):
                rows = moved[n][block * frame_blocks : (block + 1) * frame_blocks]
                wide[block_rows(block * cut.block + n), :] = rows
        for i in range(cut.tm):
            count = cut.frame_blocks * cut.rows
            x_buf[i * cut.height + j] = wide[i * count : (i + 1) * count, :].astype(BF16).reshape(cut.piece)
        return _

    pairs = every // 2
    lax.fori_loop(0, cut.height, along_time, 0)
    rows_table.wait()
    lax.fori_loop(0, cut.height, along_rows, 0)
    wait_all(load([(x_buf, out_ref)], sems))


def row_matrices(cut, taps):
    size, own = taps.shape
    near = WIDE // own
    pairs = size // near
    far = np.arange(2 * pairs - 1)[:, None, None]
    source, target = np.arange(near)[None, :, None], np.arange(near)[None, None, :]
    index = ((2 * pairs - 1 - far - pairs) * near + target - source) % size
    chosen = (index.reshape(-1, 1) == np.arange(size)[None, :]).astype(jnp.bfloat16)
    picked = jnp.dot(chosen, taps, preferred_element_type=F32).astype(BF16)
    picked = picked.reshape((2 * pairs - 1) * near, 1, WIDE)
    same = jnp.asarray(np.tile(np.eye(own), (1, near)).astype(jnp.bfloat16))
    return (picked * same[None]).reshape((2 * pairs - 1) * WIDE, WIDE)


def shards(frames_in, time_taps, row_taps):
    frames, rows, lanes = frames_in.shape
    tm, height = lax.axis_size("tm"), lax.axis_size("height")
    if not Cut.fits(frames, rows, lanes, time_taps.shape[1], tm, height):
        return narrow_shards(frames_in, time_taps, row_taps)
    width = lanes // PARTS
    cut = Cut(frames, rows, width, tm, height)
    size = frames * tm
    tables = fourier_tables(size)
    device = lax.axis_index("tm") * height + lax.axis_index("height")

    def free(*arrays):
        return [(array, ANYWHERE) for array in arrays]

    shape = (cut.devices,) + cut.piece
    sems = pltpu.SemaphoreType.DMA((RUNS * (cut.block // 2 + 2) + 8,))
    part_buf, table_buf = pltpu.VMEM((frames, rows, width), BF16), pltpu.VMEM((cut.block * TILE // FOLDS,) * 2, BF16)
    piece_buf = pltpu.VMEM(shape, BF16)
    lhs = pltpu.VMEM((FOLDS, cut.tiles * in_turn(cut)[0] * rows, cut.block * TILE // FOLDS), BF16)

    def exchange(pieces):
        flat = pieces.reshape(cut.devices, -1, TILE)
        return lax.all_to_all(flat, ("tm", "height"), 0, 0, tiled=True).reshape(shape)

    def pack(part):
        kernel = functools.partial(pack_kernel, part * width, cut)
        scratch = [part_buf, table_buf, lhs, piece_buf, sems]
        return exchange(call(kernel, free(frames_in), free(shape), scratch)[0])

    def own_lanes(taps, part):
        first = (part * width + device % cut.tiles * TILE + device // cut.tiles * cut.own) % taps.shape[1]
        return lax.dynamic_slice_in_dim(taps, first, cut.own, axis=1)

    def both(pieces, part):
        taps = jnp.tile(own_lanes(time_taps, part), (1, TILE // cut.own))
        out = ((3, size // 2, TILE), pl.BlockSpec((3, size // 2, TILE), lambda n: (0, 0, 0)))
        (spectrum,) = call(spectrum_kernel, [whole(t) for t in (taps, *tables[:2])], [out], dtype=F32, vmem=FILTER_VMEM)
        matrices = row_matrices(cut, own_lanes(row_taps, part))
        every = rows * height * cut.own
        scratch = [piece_buf, pltpu.VMEM((size, every), BF16), pltpu.VMEM(((size // cut.block + 1) * rows, TILE), F32)]
        scratch += [pltpu.VMEM((cut.row_blocks, size + cut.block, TILE), F32), pltpu.VMEM(spectrum.shape, F32)]
        scratch += [pltpu.VMEM(t.shape, BF16) for t in (*tables, matrices)] + [table_buf, sems]
        ins = free(pieces, spectrum, *tables, matrices)
        flops = 2 * size * every * (5 * size + every)
        return exchange(call(functools.partial(filter_kernel, cut), ins, free(shape), scratch, flops, vmem=FILTER_VMEM)[0])

    def unpack_add(pieces, part, held):
        kernel = functools.partial(unpack_add_kernel, part * width, cut)
        scratch = [piece_buf, part_buf, table_buf, lhs, sems]
        return call(kernel, free(pieces, frames_in), free(frames_in.shape), scratch, held=held)[0]

    arrived = [pack(part) for part in range(PARTS)]
    returned = [both(pieces, part) for part, pieces in enumerate(arrived)]
    out = None
    for part, pieces in enumerate(returned):
        out = unpack_add(pieces, part, out)
    return out


def lane_taps(tap_table, first_lane, lane_count):
    channels = tap_table.shape[1]
    distinct = min(lane_count, channels)
    lane_ids = (first_lane + lax.iota(jnp.int32, distinct)) % channels
    selector = (lane_ids[None, :] == lax.iota(jnp.int32, channels)[:, None]).astype(tap_table.dtype)
    picked = jnp.dot(tap_table, selector, preferred_element_type=jnp.float32).astype(
        tap_table.dtype
    )
    return jnp.transpose(picked)


def shifted_taps(taps, base, size):
    distinct, period = taps.shape
    start = (base - (size - 1)) % period
    tiled = jnp.concatenate([taps, taps, taps], axis=1)
    window = lax.slice_in_dim(tiled, start, start + 2 * size - 1, axis=1)
    reversed_window = window[:, ::-1]
    padded = jnp.concatenate([reversed_window, jnp.zeros((distinct, 1), taps.dtype)], axis=1)
    repeated = jnp.tile(padded, (1, size + 1))
    flat = lax.slice_in_dim(repeated, size - 1, size - 1 + size * (2 * size - 1), axis=1)
    return flat.reshape(distinct, size, 2 * size - 1)[:, :, :size]


def time_convolve(segment, own_taps):
    frames, rows_here, lane_count = segment.shape
    distinct = own_taps.shape[0]
    columns = lane_count // distinct
    block_len = min(128, frames)
    block_count = frames // block_len
    blocked = segment.reshape(block_count, block_len, rows_here, columns, distinct)
    blocked = jnp.transpose(blocked, (4, 3, 2, 0, 1))
    running = jnp.zeros((distinct, columns, rows_here, block_count, block_len), jnp.float32)
    for lag_index in range(block_count):
        toeplitz = shifted_taps(own_taps, lag_index * block_len, block_len)
        rolled = jnp.roll(blocked, lag_index, axis=3)
        running = running + jnp.einsum(
            "cab,cxrnb->cxrna", toeplitz, rolled, preferred_element_type=jnp.float32
        )
    result = jnp.transpose(running, (3, 4, 2, 1, 0)).reshape(frames, rows_here, lane_count)
    return result.astype(jnp.bfloat16)


def row_convolve(segment, row_taps):
    frames, height, lane_count = segment.shape
    distinct = row_taps.shape[0]
    columns = lane_count // distinct
    arranged = jnp.transpose(segment.reshape(frames, height, columns, distinct), (3, 2, 0, 1))
    circulant = shifted_taps(row_taps, 0, height)
    filtered = jnp.einsum("cab,cxfb->cxfa", circulant, arranged, preferred_element_type=jnp.float32)
    result = jnp.transpose(filtered, (2, 3, 1, 0)).reshape(frames, height, lane_count)
    return result.astype(jnp.bfloat16)


def narrow_shards(frames_in, time_filter, height_filter):
    frames_dev, rows_dev, lane_total = frames_in.shape
    tm_count = lax.axis_size("tm")
    height_count = lax.axis_size("height")
    lane_count = lane_total // (tm_count * height_count)
    first_lane = (
        lax.axis_index("tm") * (lane_total // tm_count) + lax.axis_index("height") * lane_count
    )
    own_taps = lane_taps(time_filter, first_lane, lane_count)
    row_taps = lane_taps(height_filter, first_lane, lane_count)
    gathered = lax.all_to_all(
        lax.all_to_all(frames_in, "tm", split_axis=2, concat_axis=0, tiled=True),
        "height",
        split_axis=2,
        concat_axis=1,
        tiled=True,
    )
    temporal = time_convolve(gathered, own_taps)
    spatial_lanes = row_convolve(temporal, row_taps)
    returned = lax.all_to_all(
        lax.all_to_all(spatial_lanes, "tm", split_axis=0, concat_axis=2, tiled=True),
        "height",
        split_axis=1,
        concat_axis=2,
        tiled=True,
    )
    spatial = returned.reshape(frames_dev, rows_dev, height_count, tm_count, lane_count)
    spatial = jnp.transpose(spatial, (0, 1, 3, 2, 4)).reshape(frames_dev, rows_dev, lane_total)
    return (frames_in.astype(jnp.float32) + spatial.astype(jnp.float32)).astype(jnp.bfloat16)


def solution(mesh):
    return jax.shard_map(
        shards,
        mesh=mesh,
        in_specs=(P("tm", "height", None), P(), P()),
        out_specs=P("tm", "height", None),
        check_vma=False,
    )
```

```python
import functools

import jax
import jax.numpy as jnp
import numpy as np
from jax import lax
from jax.experimental import pallas as pl
from jax.experimental.pallas import tpu as pltpu
from jax.sharding import PartitionSpec as P

F32, BF16 = jnp.float32, jnp.bfloat16
TILE = 128
WIDE = 2 * TILE
PARTS = 2
RUNS = 2
FOLDS = 2
VMEM_BYTES = 62 << 20
FILTER_VMEM = 40 << 20
ANYWHERE = pl.BlockSpec(memory_space=pl.ANY)


def split_terms(table):
    high = table.astype(jnp.bfloat16)
    low = (table - high.astype(np.float64)).astype(jnp.bfloat16)
    return high, low


def fourier_tables(size):
    half = size // 2
    wave, at = np.arange(half)[:, None], np.arange(size)[None, :]
    angle = 2.0 * np.pi * ((wave * at) % size) / size
    sines = np.sin(angle)
    sines[0] = 1.0 - 2.0 * (np.arange(size) % 2)
    analysis = np.concatenate([np.cos(angle), sines], axis=0)
    weight = np.full((size,), 2.0 / size)
    weight[0] = weight[half] = 1.0 / size
    synthesis = (analysis * weight[:, None]).T
    return split_terms(analysis) + split_terms(synthesis)


def spectrum_kernel(taps_ref, high_ref, low_ref, out_ref):
    half = taps_ref.shape[0] // 2
    sums = jnp.dot(high_ref[...], taps_ref[...], preferred_element_type=F32)
    sums += jnp.dot(low_ref[...], taps_ref[...], preferred_element_type=F32)
    cosines, sines = sums[:half], sums[half:]
    first = lax.broadcasted_iota(jnp.int32, cosines.shape, 0) == 0
    out_ref[0] = cosines
    out_ref[1] = jnp.where(first, 0.0, sines)
    out_ref[2] = jnp.where(first, sines, cosines)


def filtered(signal, spectrum, tables):
    half = spectrum.shape[1]
    analysis_high, analysis_low, synthesis_high, synthesis_low = (t[...] for t in tables)
    coef = jnp.dot(analysis_high, signal, preferred_element_type=F32)
    coef += jnp.dot(analysis_low, signal, preferred_element_type=F32)
    cos_part, sin_part = coef[:half], coef[half:]
    keep, turn, other = (jnp.concatenate([spectrum[n]] * (signal.shape[1] // TILE), axis=1) for n in range(3))
    product = jnp.concatenate([cos_part * keep - sin_part * turn, sin_part * other + cos_part * turn], axis=0)
    high = product.astype(BF16)
    low = (product - high.astype(F32)).astype(BF16)
    result = jnp.dot(synthesis_high, high, preferred_element_type=F32)
    result += jnp.dot(synthesis_low, high, preferred_element_type=F32)
    result += jnp.dot(synthesis_high, low, preferred_element_type=F32)
    return result


class Cut:
    def __init__(self, frames, rows, width, tm, height):
        self.frames, self.rows, self.width, self.tm, self.height = frames, rows, width, tm, height
        self.devices = tm * height
        self.own = width // self.devices
        self.block = TILE // self.own
        self.frame_blocks, self.row_blocks = frames // self.block, rows // self.block
        self.tiles = width // TILE
        self.piece = (self.frame_blocks, rows, TILE)

    @staticmethod
    def fits(frames, rows, lanes, channels, tm, height):
        own = lanes // PARTS // (tm * height)
        if own == 0 or TILE % own or lanes != PARTS * own * tm * height or lanes // PARTS % TILE or channels % own:
            return False
        block = TILE // own
        return frames % block == 0 and rows % block == 0 and rows % 16 == 0 and rows // block % 2 == 0 and block % (2 * FOLDS) == 0


def call(kernel, ins, outs, scratch=(), flops=0, held=None, dtype=BF16, vmem=VMEM_BYTES):
    unread = [] if held is None else [held]

    def body(*refs):
        kernel(*refs[: len(ins)], *refs[len(ins) + len(unread) :])

    moved = 2 * sum(int(np.prod(a.shape)) for a, _ in ins) + 2 * sum(int(np.prod(s)) for s, _ in outs)
    return pl.pallas_call(
        body,
        grid=(1,),
        in_specs=[spec for _, spec in ins] + [ANYWHERE] * len(unread),
        out_specs=[spec for _, spec in outs],
        out_shape=[jax.ShapeDtypeStruct(shape, dtype) for shape, _ in outs],
        scratch_shapes=list(scratch),
        input_output_aliases={} if held is None else {len(ins): 0},
        compiler_params=pltpu.CompilerParams(vmem_limit_bytes=vmem),
        cost_estimate=pl.CostEstimate(flops=flops, bytes_accessed=moved, transcendentals=0),
    )(*[array for array, _ in ins], *unread)


def whole(table):
    return table, pl.BlockSpec(table.shape, lambda n: (0,) * table.ndim)


def start_all(copies):
    for copy in copies:
        copy.start()
    return copies


def wait_all(copies):
    for copy in copies:
        copy.wait()


def load(pairs, sems, first=0):
    return start_all([pltpu.make_async_copy(a, b, sems.at[first + n]) for n, (a, b) in enumerate(pairs)])


def fill_shuffle(cut, shuffle):
    row = lax.broadcasted_iota(jnp.int32, shuffle.shape, 0)
    column = lax.broadcasted_iota(jnp.int32, (1, shuffle.shape[1]), 1)
    m, n, lane = column // TILE, column % TILE // cut.own, column % cut.own
    shuffle[...] = (row == n * (TILE // FOLDS) + m * cut.own + lane).astype(F32).astype(BF16)


def folds(tiles):
    for fold in range(FOLDS):
        lanes = slice(fold * TILE // FOLDS, (fold + 1) * TILE // FOLDS)
        yield [
            jnp.concatenate([tile[:, lanes] for tile in tiles[n : n + FOLDS]], axis=1)
            for n in range(0, len(tiles), FOLDS)
        ]


def shuffled(tiles, shuffle):
    result = []
    for part in folds(tiles):
        moved = jnp.dot(jnp.concatenate(part, axis=1), shuffle[...], preferred_element_type=F32)
        result += [moved[:, m * TILE : (m + 1) * TILE] for m in range(len(tiles) // FOLDS)]
    return result


def lay_out(tiles, lhs, rows):
    for fold, part in enumerate(folds(tiles)):
        for n, tile in enumerate(part):
            lhs[fold, rows, n * TILE : (n + 1) * TILE] = tile


def in_turn(cut):
    count = next(n for n in (RUNS, 1) if cut.frame_blocks % n == 0)
    step = cut.frame_blocks // count
    return step, range(0, cut.frame_blocks, step), range(0, cut.block, 2)


def exchange_lanes(cut, step, lhs, shuffle, first):
    fold, at = divmod(first, cut.block // FOLDS)
    moved = jnp.dot(lhs[fold], shuffle[:, at * TILE : (at + 2) * TILE], preferred_element_type=F32)
    shape = (cut.tiles, step, cut.rows, TILE)
    return [(first + n, moved[:, n * TILE : (n + 1) * TILE].reshape(shape)) for n in range(2)]


def pack_kernel(lane, cut, x_ref, out_ref, x_buf, shuffle, lhs, out_buf, sems):
    step, runs, pairs = in_turn(cut)
    size = step * cut.rows
    frames = [pl.ds(run * cut.block, step * cut.block) for run in runs]
    arriving = load([(x_ref.at[at, :, pl.ds(lane, cut.width)], x_buf.at[at]) for at in frames], sems)
    fill_shuffle(cut, shuffle)
    leaving = []
    for turn, run in enumerate(runs):
        arriving[turn].wait()
        for tile in range(cut.tiles):
            lanes = slice(tile * TILE, (tile + 1) * TILE)
            x = x_buf[frames[turn], :, lanes].reshape(step, cut.block, cut.rows, TILE)
            lay_out([x[:, n].reshape(size, TILE) for n in range(cut.block)], lhs, slice(tile * size, (tile + 1) * size))
        for pair in pairs:
            for m, piece in exchange_lanes(cut, step, lhs, shuffle, pair):
                for tile in range(cut.tiles):
                    out_buf[m * cut.tiles + tile, run : run + step] = piece[tile].astype(BF16)
            count = cut.block // FOLDS
            if (pair + 2) % count == 0:
                some = (pl.ds((pair + 2 - count) * cut.tiles, count * cut.tiles), pl.ds(run, step))
                leaving += load([(out_buf.at[some], out_ref.at[some])], sems, len(runs) + len(leaving))
    wait_all(leaving)


def unpack_add_kernel(lane, cut, y_ref, x_ref, out_ref, y_buf, x_buf, shuffle, lhs, sems):
    step, runs, pairs = in_turn(cut)
    size = step * cut.rows
    lanes = pl.ds(lane, cut.width)
    parts = [pl.ds(run, step) for run in runs]
    frames = [pl.ds(run * cut.block, step * cut.block) for run in runs]
    arriving, added = [], []
    for turn, (part, at) in enumerate(zip(parts, frames)):
        arriving += load([(y_ref.at[:, part], y_buf.at[:, part])], sems, turn)
        added += load([(x_ref.at[at, :, lanes], x_buf.at[at])], sems, RUNS + turn)
    fill_shuffle(cut, shuffle)
    leaving = []
    for turn, run in enumerate(runs):
        arriving[turn].wait()
        for tile in range(cut.tiles):
            y = [y_buf[m * cut.tiles + tile, run : run + step].reshape(size, TILE) for m in range(cut.block)]
            lay_out(y, lhs, slice(tile * size, (tile + 1) * size))
        added[turn].wait()
        for pair in pairs:
            for n, piece in exchange_lanes(cut, step, lhs, shuffle, pair):
                for tile in range(cut.tiles):
                    for block in range(step):
                        frame, at = (run + block) * cut.block + n, slice(tile * TILE, (tile + 1) * TILE)
                        x_buf[frame, :, at] = (x_buf[frame, :, at].astype(F32) + piece[tile, block]).astype(BF16)
        leaving += load([(x_buf.at[frames[turn]], out_ref.at[frames[turn], :, lanes])], sems, 2 * RUNS + turn)
    wait_all(leaving)


def filter_kernel(cut, x_ref, spectrum_ref, analysis_h, analysis_l, synthesis_h, synthesis_l, rows_ref, *refs):
    out_ref, x_buf, temporal, wide, column, spectrum, *tables, row_table, shuffle, sems = refs
    every = cut.height * cut.row_blocks
    frame_blocks = cut.tm * cut.frame_blocks
    size = cut.tm * cut.frames
    arriving = load([(x_ref, x_buf), (spectrum_ref, spectrum)], sems)
    arriving += load(zip((analysis_h, analysis_l, synthesis_h, synthesis_l), tables), sems, 2)
    (rows_table,) = load([(rows_ref, row_table)], sems, 2 + len(tables))
    fill_shuffle(cut, shuffle)
    wait_all(arriving)

    def block_rows(n):
        return pl.ds(n, frame_blocks, stride=cut.rows)

    def block_frames(n):
        return pl.ds(n, frame_blocks, stride=cut.block)

    def along_time(j, _):
        for i in range(cut.tm):
            piece = x_buf[i * cut.height + j].astype(F32).reshape(-1, TILE)
            wide[i * piece.shape[0] : (i + 1) * piece.shape[0], :] = piece
        parts = [
            jnp.concatenate(
                [wide[block_rows(block * cut.block + n), :].astype(BF16) for block in range(cut.row_blocks)], axis=0
            )
            for n in range(cut.block)
        ]
        moved = shuffled(parts, shuffle)
        for block in range(cut.row_blocks):
            for n in range(cut.block):
                column[block, block_frames(n), :] = moved[n][block * frame_blocks : (block + 1) * frame_blocks]
        for block in range(0, cut.row_blocks, 2):
            signal = jnp.concatenate([column[block + n, :size].astype(BF16) for n in range(2)], axis=1)
            at = pl.ds(pl.multiple_of((j * cut.row_blocks + block) * TILE, WIDE), WIDE)
            temporal[:, at] = filtered(signal, spectrum[...], tables).astype(BF16)
        return _

    def along_rows(j, _):
        for block in range(0, cut.row_blocks, 2):
            first = pairs - 1 - (j * cut.row_blocks + block) // 2
            matrix = row_table[pl.ds(pl.multiple_of(first * WIDE, WIDE), pairs * WIDE), :]
            result = jnp.dot(temporal[...], matrix, preferred_element_type=F32)
            column[block, :size], column[block + 1, :size] = result[:, :TILE], result[:, TILE:]
        parts = [
            jnp.concatenate([column[block, block_frames(n), :].astype(BF16) for block in range(cut.row_blocks)], axis=0)
            for n in range(cut.block)
        ]
        moved = shuffled(parts, shuffle)
        for block in range(cut.row_blocks):
            for n in range(cut.block):
                rows = moved[n][block * frame_blocks : (block + 1) * frame_blocks]
                wide[block_rows(block * cut.block + n), :] = rows
        for i in range(cut.tm):
            count = cut.frame_blocks * cut.rows
            x_buf[i * cut.height + j] = wide[i * count : (i + 1) * count, :].astype(BF16).reshape(cut.piece)
        return _

    pairs = every // 2
    lax.fori_loop(0, cut.height, along_time, 0)
    rows_table.wait()
    lax.fori_loop(0, cut.height, along_rows, 0)
    wait_all(load([(x_buf, out_ref)], sems))


def row_matrices(cut, taps):
    size, own = taps.shape
    near = WIDE // own
    pairs = size // near
    far = np.arange(2 * pairs - 1)[:, None, None]
    source, target = np.arange(near)[None, :, None], np.arange(near)[None, None, :]
    index = ((2 * pairs - 1 - far - pairs) * near + target - source) % size
    chosen = (index.reshape(-1, 1) == np.arange(size)[None, :]).astype(jnp.bfloat16)
    picked = jnp.dot(chosen, taps, preferred_element_type=F32).astype(BF16)
    picked = picked.reshape((2 * pairs - 1) * near, 1, WIDE)
    same = jnp.asarray(np.tile(np.eye(own), (1, near)).astype(jnp.bfloat16))
    return (picked * same[None]).reshape((2 * pairs - 1) * WIDE, WIDE)


def shards(frames_in, time_taps, row_taps):
    frames, rows, lanes = frames_in.shape
    tm, height = lax.axis_size("tm"), lax.axis_size("height")
    if not Cut.fits(frames, rows, lanes, time_taps.shape[1], tm, height):
        return narrow_shards(frames_in, time_taps, row_taps)
    width = lanes // PARTS
    cut = Cut(frames, rows, width, tm, height)
    size = frames * tm
    tables = fourier_tables(size)
    device = lax.axis_index("tm") * height + lax.axis_index("height")

    def free(*arrays):
        return [(array, ANYWHERE) for array in arrays]

    shape = (cut.devices,) + cut.piece
    sems = pltpu.SemaphoreType.DMA((max(RUNS * (1 + FOLDS), 3 * RUNS, 7),))
    part_buf, table_buf = pltpu.VMEM((frames, rows, width), BF16), pltpu.VMEM((cut.block * TILE // FOLDS,) * 2, BF16)
    piece_buf = pltpu.VMEM(shape, BF16)
    lhs = pltpu.VMEM((FOLDS, cut.tiles * in_turn(cut)[0] * rows, cut.block * TILE // FOLDS), BF16)

    def exchange(pieces):
        flat = pieces.reshape(cut.devices, -1, TILE)
        return lax.all_to_all(flat, ("tm", "height"), 0, 0, tiled=True).reshape(shape)

    def pack(part):
        kernel = functools.partial(pack_kernel, part * width, cut)
        scratch = [part_buf, table_buf, lhs, piece_buf, sems]
        return exchange(call(kernel, free(frames_in), free(shape), scratch)[0])

    def own_lanes(taps, part):
        first = (part * width + device % cut.tiles * TILE + device // cut.tiles * cut.own) % taps.shape[1]
        return lax.dynamic_slice_in_dim(taps, first, cut.own, axis=1)

    def both(pieces, part):
        taps = jnp.tile(own_lanes(time_taps, part), (1, TILE // cut.own))
        out = ((3, size // 2, TILE), pl.BlockSpec((3, size // 2, TILE), lambda n: (0, 0, 0)))
        (spectrum,) = call(spectrum_kernel, [whole(t) for t in (taps, *tables[:2])], [out], dtype=F32, vmem=FILTER_VMEM)
        matrices = row_matrices(cut, own_lanes(row_taps, part))
        every = rows * height * cut.own
        scratch = [piece_buf, pltpu.VMEM((size, every), BF16), pltpu.VMEM(((size // cut.block + 1) * rows, TILE), F32)]
        scratch += [pltpu.VMEM((cut.row_blocks, size + cut.block, TILE), F32), pltpu.VMEM(spectrum.shape, F32)]
        scratch += [pltpu.VMEM(t.shape, BF16) for t in (*tables, matrices)] + [table_buf, sems]
        ins = free(pieces, spectrum, *tables, matrices)
        flops = 2 * size * every * (5 * size + every)
        return exchange(call(functools.partial(filter_kernel, cut), ins, free(shape), scratch, flops, vmem=FILTER_VMEM)[0])

    def unpack_add(pieces, part, held):
        kernel = functools.partial(unpack_add_kernel, part * width, cut)
        scratch = [piece_buf, part_buf, table_buf, lhs, sems]
        return call(kernel, free(pieces, frames_in), free(frames_in.shape), scratch, held=held)[0]

    arrived = [pack(part) for part in range(PARTS)]
    returned = [both(pieces, part) for part, pieces in enumerate(arrived)]
    out = None
    for part, pieces in enumerate(returned):
        out = unpack_add(pieces, part, out)
    return out


def lane_taps(tap_table, first_lane, lane_count):
    channels = tap_table.shape[1]
    distinct = min(lane_count, channels)
    lane_ids = (first_lane + lax.iota(jnp.int32, distinct)) % channels
    selector = (lane_ids[None, :] == lax.iota(jnp.int32, channels)[:, None]).astype(tap_table.dtype)
    picked = jnp.dot(tap_table, selector, preferred_element_type=jnp.float32).astype(
        tap_table.dtype
    )
    return jnp.transpose(picked)


def shifted_taps(taps, base, size):
    distinct, period = taps.shape
    start = (base - (size - 1)) % period
    tiled = jnp.concatenate([taps, taps, taps], axis=1)
    window = lax.slice_in_dim(tiled, start, start + 2 * size - 1, axis=1)
    reversed_window = window[:, ::-1]
    padded = jnp.concatenate([reversed_window, jnp.zeros((distinct, 1), taps.dtype)], axis=1)
    repeated = jnp.tile(padded, (1, size + 1))
    flat = lax.slice_in_dim(repeated, size - 1, size - 1 + size * (2 * size - 1), axis=1)
    return flat.reshape(distinct, size, 2 * size - 1)[:, :, :size]


def time_convolve(segment, own_taps):
    frames, rows_here, lane_count = segment.shape
    distinct = own_taps.shape[0]
    columns = lane_count // distinct
    block_len = min(128, frames)
    block_count = frames // block_len
    blocked = segment.reshape(block_count, block_len, rows_here, columns, distinct)
    blocked = jnp.transpose(blocked, (4, 3, 2, 0, 1))
    running = jnp.zeros((distinct, columns, rows_here, block_count, block_len), jnp.float32)
    for lag_index in range(block_count):
        toeplitz = shifted_taps(own_taps, lag_index * block_len, block_len)
        rolled = jnp.roll(blocked, lag_index, axis=3)
        running = running + jnp.einsum(
            "cab,cxrnb->cxrna", toeplitz, rolled, preferred_element_type=jnp.float32
        )
    result = jnp.transpose(running, (3, 4, 2, 1, 0)).reshape(frames, rows_here, lane_count)
    return result.astype(jnp.bfloat16)


def row_convolve(segment, row_taps):
    frames, height, lane_count = segment.shape
    distinct = row_taps.shape[0]
    columns = lane_count // distinct
    arranged = jnp.transpose(segment.reshape(frames, height, columns, distinct), (3, 2, 0, 1))
    circulant = shifted_taps(row_taps, 0, height)
    filtered = jnp.einsum("cab,cxfb->cxfa", circulant, arranged, preferred_element_type=jnp.float32)
    result = jnp.transpose(filtered, (2, 3, 1, 0)).reshape(frames, height, lane_count)
    return result.astype(jnp.bfloat16)


def narrow_shards(frames_in, time_filter, height_filter):
    frames_dev, rows_dev, lane_total = frames_in.shape
    tm_count = lax.axis_size("tm")
    height_count = lax.axis_size("height")
    lane_count = lane_total // (tm_count * height_count)
    first_lane = (
        lax.axis_index("tm") * (lane_total // tm_count) + lax.axis_index("height") * lane_count
    )
    own_taps = lane_taps(time_filter, first_lane, lane_count)
    row_taps = lane_taps(height_filter, first_lane, lane_count)
    gathered = lax.all_to_all(
        lax.all_to_all(frames_in, "tm", split_axis=2, concat_axis=0, tiled=True),
        "height",
        split_axis=2,
        concat_axis=1,
        tiled=True,
    )
    temporal = time_convolve(gathered, own_taps)
    spatial_lanes = row_convolve(temporal, row_taps)
    returned = lax.all_to_all(
        lax.all_to_all(spatial_lanes, "tm", split_axis=0, concat_axis=2, tiled=True),
        "height",
        split_axis=1,
        concat_axis=2,
        tiled=True,
    )
    spatial = returned.reshape(frames_dev, rows_dev, height_count, tm_count, lane_count)
    spatial = jnp.transpose(spatial, (0, 1, 3, 2, 4)).reshape(frames_dev, rows_dev, lane_total)
    return (frames_in.astype(jnp.float32) + spatial.astype(jnp.float32)).astype(jnp.bfloat16)


def solution(mesh):
    return jax.shard_map(
        shards,
        mesh=mesh,
        in_specs=(P("tm", "height", None), P(), P()),
        out_specs=P("tm", "height", None),
        check_vma=False,
    )
```

```python
import functools

import jax
import jax.numpy as jnp
import numpy as np
from jax import lax
from jax.experimental import pallas as pl
from jax.experimental.pallas import tpu as pltpu
from jax.sharding import PartitionSpec as P

F32, BF16 = jnp.float32, jnp.bfloat16
TILE = 128
WIDE = 2 * TILE
PARTS = 2
RUNS = 2
EARLY = 4
FOLDS = 2
VMEM_BYTES = 62 << 20
FILTER_VMEM = 40 << 20
ANYWHERE = pl.BlockSpec(memory_space=pl.ANY)


def split_terms(table):
    high = table.astype(jnp.bfloat16)
    low = (table - high.astype(np.float64)).astype(jnp.bfloat16)
    return high, low


def fourier_tables(size):
    half = size // 2
    wave, at = np.arange(half)[:, None], np.arange(size)[None, :]
    angle = 2.0 * np.pi * ((wave * at) % size) / size
    sines = np.sin(angle)
    sines[0] = 1.0 - 2.0 * (np.arange(size) % 2)
    analysis = np.concatenate([np.cos(angle), sines], axis=0)
    weight = np.full((size,), 2.0 / size)
    weight[0] = weight[half] = 1.0 / size
    synthesis = (analysis * weight[:, None]).T
    return split_terms(analysis) + split_terms(synthesis)


def spectrum_kernel(taps_ref, high_ref, low_ref, out_ref):
    half = taps_ref.shape[0] // 2
    sums = jnp.dot(high_ref[...], taps_ref[...], preferred_element_type=F32)
    sums += jnp.dot(low_ref[...], taps_ref[...], preferred_element_type=F32)
    cosines, sines = sums[:half], sums[half:]
    first = lax.broadcasted_iota(jnp.int32, cosines.shape, 0) == 0
    out_ref[0] = cosines
    out_ref[1] = jnp.where(first, 0.0, sines)
    out_ref[2] = jnp.where(first, sines, cosines)


def filtered(signal, spectrum, tables):
    half = spectrum.shape[1]
    analysis_high, analysis_low, synthesis_high, synthesis_low = (t[...] for t in tables)
    coef = jnp.dot(analysis_high, signal, preferred_element_type=F32)
    coef += jnp.dot(analysis_low, signal, preferred_element_type=F32)
    cos_part, sin_part = coef[:half], coef[half:]
    keep, turn, other = (jnp.concatenate([spectrum[n]] * (signal.shape[1] // TILE), axis=1) for n in range(3))
    product = jnp.concatenate([cos_part * keep - sin_part * turn, sin_part * other + cos_part * turn], axis=0)
    high = product.astype(BF16)
    low = (product - high.astype(F32)).astype(BF16)
    result = jnp.dot(synthesis_high, high, preferred_element_type=F32)
    result += jnp.dot(synthesis_low, high, preferred_element_type=F32)
    result += jnp.dot(synthesis_high, low, preferred_element_type=F32)
    return result


class Cut:
    def __init__(self, frames, rows, width, tm, height):
        self.frames, self.rows, self.width, self.tm, self.height = frames, rows, width, tm, height
        self.devices = tm * height
        self.own = width // self.devices
        self.block = TILE // self.own
        self.frame_blocks, self.row_blocks = frames // self.block, rows // self.block
        self.tiles = width // TILE
        self.piece = (self.frame_blocks, rows, TILE)

    @staticmethod
    def fits(frames, rows, lanes, channels, tm, height):
        own = lanes // PARTS // (tm * height)
        if own == 0 or TILE % own or lanes != PARTS * own * tm * height or lanes // PARTS % TILE or channels % own:
            return False
        block = TILE // own
        return frames % block == 0 and rows % block == 0 and rows % 16 == 0 and rows // block % 2 == 0 and block % (2 * FOLDS) == 0


def call(kernel, ins, outs, scratch=(), flops=0, held=None, dtype=BF16, vmem=VMEM_BYTES):
    unread = [] if held is None else [held]

    def body(*refs):
        kernel(*refs[: len(ins)], *refs[len(ins) + len(unread) :])

    moved = 2 * sum(int(np.prod(a.shape)) for a, _ in ins) + 2 * sum(int(np.prod(s)) for s, _ in outs)
    return pl.pallas_call(
        body,
        grid=(1,),
        in_specs=[spec for _, spec in ins] + [ANYWHERE] * len(unread),
        out_specs=[spec for _, spec in outs],
        out_shape=[jax.ShapeDtypeStruct(shape, dtype) for shape, _ in outs],
        scratch_shapes=list(scratch),
        input_output_aliases={} if held is None else {len(ins): 0},
        compiler_params=pltpu.CompilerParams(vmem_limit_bytes=vmem),
        cost_estimate=pl.CostEstimate(flops=flops, bytes_accessed=moved, transcendentals=0),
    )(*[array for array, _ in ins], *unread)


def whole(table):
    return table, pl.BlockSpec(table.shape, lambda n: (0,) * table.ndim)


def start_all(copies):
    for copy in copies:
        copy.start()
    return copies


def wait_all(copies):
    for copy in copies:
        copy.wait()


def load(pairs, sems, first=0):
    return start_all([pltpu.make_async_copy(a, b, sems.at[first + n]) for n, (a, b) in enumerate(pairs)])


def fill_shuffle(cut, shuffle):
    row = lax.broadcasted_iota(jnp.int32, shuffle.shape, 0)
    column = lax.broadcasted_iota(jnp.int32, (1, shuffle.shape[1]), 1)
    m, n, lane = column // TILE, column % TILE // cut.own, column % cut.own
    shuffle[...] = (row == n * (TILE // FOLDS) + m * cut.own + lane).astype(F32).astype(BF16)


def folds(tiles):
    for fold in range(FOLDS):
        lanes = slice(fold * TILE // FOLDS, (fold + 1) * TILE // FOLDS)
        yield [
            jnp.concatenate([tile[:, lanes] for tile in tiles[n : n + FOLDS]], axis=1)
            for n in range(0, len(tiles), FOLDS)
        ]


def shuffled(tiles, shuffle):
    result = []
    for part in folds(tiles):
        moved = jnp.dot(jnp.concatenate(part, axis=1), shuffle[...], preferred_element_type=F32)
        result += [moved[:, m * TILE : (m + 1) * TILE] for m in range(len(tiles) // FOLDS)]
    return result


def lay_out(tiles, lhs, rows):
    for fold, part in enumerate(folds(tiles)):
        for n, tile in enumerate(part):
            lhs[fold, rows, n * TILE : (n + 1) * TILE] = tile


def in_turn(cut):
    early = cut.frame_blocks // EARLY
    return [run for run in ((0, early), (early, cut.frame_blocks - early)) if run[1]], range(0, cut.block, 2)


def exchange_lanes(cut, step, lhs, shuffle, first):
    fold, at = divmod(first, cut.block // FOLDS)
    moved = jnp.dot(lhs[fold, : cut.tiles * step * cut.rows], shuffle[:, at * TILE : (at + 2) * TILE], preferred_element_type=F32)
    shape = (cut.tiles, step, cut.rows, TILE)
    return [(first + n, moved[:, n * TILE : (n + 1) * TILE].reshape(shape)) for n in range(2)]


def pack_kernel(lane, cut, x_ref, out_ref, x_buf, shuffle, lhs, out_buf, sems):
    runs, pairs = in_turn(cut)
    frames = [pl.ds(run * cut.block, step * cut.block) for run, step in runs]
    arriving = load([(x_ref.at[at, :, pl.ds(lane, cut.width)], x_buf.at[at]) for at in frames], sems)
    fill_shuffle(cut, shuffle)
    leaving = []
    for turn, (run, step) in enumerate(runs):
        size = step * cut.rows
        arriving[turn].wait()
        for tile in range(cut.tiles):
            lanes = slice(tile * TILE, (tile + 1) * TILE)
            x = x_buf[frames[turn], :, lanes].reshape(step, cut.block, cut.rows, TILE)
            lay_out([x[:, n].reshape(size, TILE) for n in range(cut.block)], lhs, slice(tile * size, (tile + 1) * size))
        for pair in pairs:
            for m, piece in exchange_lanes(cut, step, lhs, shuffle, pair):
                for tile in range(cut.tiles):
                    out_buf[m * cut.tiles + tile, run : run + step] = piece[tile].astype(BF16)
            count = cut.block // FOLDS
            if (pair + 2) % count == 0:
                some = (pl.ds((pair + 2 - count) * cut.tiles, count * cut.tiles), pl.ds(run, step))
                leaving += load([(out_buf.at[some], out_ref.at[some])], sems, len(runs) + len(leaving))
    wait_all(leaving)


def unpack_add_kernel(lane, cut, y_ref, x_ref, out_ref, y_buf, x_buf, shuffle, lhs, sems):
    runs, pairs = in_turn(cut)
    lanes = pl.ds(lane, cut.width)
    parts = [pl.ds(run, step) for run, step in runs]
    frames = [pl.ds(run * cut.block, step * cut.block) for run, step in runs]
    arriving, added = [], []
    for turn, (part, at) in enumerate(zip(parts, frames)):
        arriving += load([(y_ref.at[:, part], y_buf.at[:, part])], sems, turn)
        added += load([(x_ref.at[at, :, lanes], x_buf.at[at])], sems, RUNS + turn)
    fill_shuffle(cut, shuffle)
    leaving = []
    for turn, (run, step) in enumerate(runs):
        size = step * cut.rows
        arriving[turn].wait()
        for tile in range(cut.tiles):
            y = [y_buf[m * cut.tiles + tile, run : run + step].reshape(size, TILE) for m in range(cut.block)]
            lay_out(y, lhs, slice(tile * size, (tile + 1) * size))
        added[turn].wait()
        for pair in pairs:
            for n, piece in exchange_lanes(cut, step, lhs, shuffle, pair):
                for tile in range(cut.tiles):
                    for block in range(step):
                        frame, at = (run + block) * cut.block + n, slice(tile * TILE, (tile + 1) * TILE)
                        x_buf[frame, :, at] = (x_buf[frame, :, at].astype(F32) + piece[tile, block]).astype(BF16)
        leaving += load([(x_buf.at[frames[turn]], out_ref.at[frames[turn], :, lanes])], sems, 2 * RUNS + turn)
    wait_all(leaving)


def filter_kernel(cut, x_ref, spectrum_ref, analysis_h, analysis_l, synthesis_h, synthesis_l, rows_ref, *refs):
    out_ref, x_buf, temporal, wide, column, spectrum, *tables, row_table, shuffle, sems = refs
    every = cut.height * cut.row_blocks
    frame_blocks = cut.tm * cut.frame_blocks
    size = cut.tm * cut.frames
    arriving = load([(x_ref, x_buf), (spectrum_ref, spectrum)], sems)
    arriving += load(zip((analysis_h, analysis_l, synthesis_h, synthesis_l), tables), sems, 2)
    (rows_table,) = load([(rows_ref, row_table)], sems, 2 + len(tables))
    fill_shuffle(cut, shuffle)
    wait_all(arriving)

    def block_rows(n):
        return pl.ds(n, frame_blocks, stride=cut.rows)

    def block_frames(n):
        return pl.ds(n, frame_blocks, stride=cut.block)

    def along_time(j, _):
        for i in range(cut.tm):
            piece = x_buf[i * cut.height + j].astype(F32).reshape(-1, TILE)
            wide[i * piece.shape[0] : (i + 1) * piece.shape[0], :] = piece
        parts = [
            jnp.concatenate(
                [wide[block_rows(block * cut.block + n), :].astype(BF16) for block in range(cut.row_blocks)], axis=0
            )
            for n in range(cut.block)
        ]
        moved = shuffled(parts, shuffle)
        for block in range(cut.row_blocks):
            for n in range(cut.block):
                column[block, block_frames(n), :] = moved[n][block * frame_blocks : (block + 1) * frame_blocks]
        for block in range(0, cut.row_blocks, 2):
            signal = jnp.concatenate([column[block + n, :size].astype(BF16) for n in range(2)], axis=1)
            at = pl.ds(pl.multiple_of((j * cut.row_blocks + block) * TILE, WIDE), WIDE)
            temporal[:, at] = filtered(signal, spectrum[...], tables).astype(BF16)
        return _

    def along_rows(j, _):
        for block in range(0, cut.row_blocks, 2):
            first = pairs - 1 - (j * cut.row_blocks + block) // 2
            matrix = row_table[pl.ds(pl.multiple_of(first * WIDE, WIDE), pairs * WIDE), :]
            result = jnp.dot(temporal[...], matrix, preferred_element_type=F32)
            column[block, :size], column[block + 1, :size] = result[:, :TILE], result[:, TILE:]
        parts = [
            jnp.concatenate([column[block, block_frames(n), :].astype(BF16) for block in range(cut.row_blocks)], axis=0)
            for n in range(cut.block)
        ]
        moved = shuffled(parts, shuffle)
        for block in range(cut.row_blocks):
            for n in range(cut.block):
                rows = moved[n][block * frame_blocks : (block + 1) * frame_blocks]
                wide[block_rows(block * cut.block + n), :] = rows
        for i in range(cut.tm):
            count = cut.frame_blocks * cut.rows
            x_buf[i * cut.height + j] = wide[i * count : (i + 1) * count, :].astype(BF16).reshape(cut.piece)
        return _

    pairs = every // 2
    lax.fori_loop(0, cut.height, along_time, 0)
    rows_table.wait()
    lax.fori_loop(0, cut.height, along_rows, 0)
    wait_all(load([(x_buf, out_ref)], sems))


def row_matrices(cut, taps):
    size, own = taps.shape
    near = WIDE // own
    pairs = size // near
    far = np.arange(2 * pairs - 1)[:, None, None]
    source, target = np.arange(near)[None, :, None], np.arange(near)[None, None, :]
    index = ((2 * pairs - 1 - far - pairs) * near + target - source) % size
    chosen = (index.reshape(-1, 1) == np.arange(size)[None, :]).astype(jnp.bfloat16)
    picked = jnp.dot(chosen, taps, preferred_element_type=F32).astype(BF16)
    picked = picked.reshape((2 * pairs - 1) * near, 1, WIDE)
    same = jnp.asarray(np.tile(np.eye(own), (1, near)).astype(jnp.bfloat16))
    return (picked * same[None]).reshape((2 * pairs - 1) * WIDE, WIDE)


def shards(frames_in, time_taps, row_taps):
    frames, rows, lanes = frames_in.shape
    tm, height = lax.axis_size("tm"), lax.axis_size("height")
    if not Cut.fits(frames, rows, lanes, time_taps.shape[1], tm, height):
        return narrow_shards(frames_in, time_taps, row_taps)
    width = lanes // PARTS
    cut = Cut(frames, rows, width, tm, height)
    size = frames * tm
    tables = fourier_tables(size)
    device = lax.axis_index("tm") * height + lax.axis_index("height")

    def free(*arrays):
        return [(array, ANYWHERE) for array in arrays]

    shape = (cut.devices,) + cut.piece
    sems = pltpu.SemaphoreType.DMA((max(RUNS * (1 + FOLDS), 3 * RUNS, 7),))
    part_buf, table_buf = pltpu.VMEM((frames, rows, width), BF16), pltpu.VMEM((cut.block * TILE // FOLDS,) * 2, BF16)
    piece_buf = pltpu.VMEM(shape, BF16)
    lhs = pltpu.VMEM((FOLDS, cut.tiles * max(n for _, n in in_turn(cut)[0]) * rows, cut.block * TILE // FOLDS), BF16)

    def exchange(pieces):
        flat = pieces.reshape(cut.devices, -1, TILE)
        return lax.all_to_all(flat, ("tm", "height"), 0, 0, tiled=True).reshape(shape)

    def pack(part):
        kernel = functools.partial(pack_kernel, part * width, cut)
        scratch = [part_buf, table_buf, lhs, piece_buf, sems]
        return exchange(call(kernel, free(frames_in), free(shape), scratch)[0])

    def own_lanes(taps, part):
        first = (part * width + device % cut.tiles * TILE + device // cut.tiles * cut.own) % taps.shape[1]
        return lax.dynamic_slice_in_dim(taps, first, cut.own, axis=1)

    def both(pieces, part):
        taps = jnp.tile(own_lanes(time_taps, part), (1, TILE // cut.own))
        out = ((3, size // 2, TILE), pl.BlockSpec((3, size // 2, TILE), lambda n: (0, 0, 0)))
        (spectrum,) = call(spectrum_kernel, [whole(t) for t in (taps, *tables[:2])], [out], dtype=F32, vmem=FILTER_VMEM)
        matrices = row_matrices(cut, own_lanes(row_taps, part))
        every = rows * height * cut.own
        scratch = [piece_buf, pltpu.VMEM((size, every), BF16), pltpu.VMEM(((size // cut.block + 1) * rows, TILE), F32)]
        scratch += [pltpu.VMEM((cut.row_blocks, size + cut.block, TILE), F32), pltpu.VMEM(spectrum.shape, F32)]
        scratch += [pltpu.VMEM(t.shape, BF16) for t in (*tables, matrices)] + [table_buf, sems]
        ins = free(pieces, spectrum, *tables, matrices)
        flops = 2 * size * every * (5 * size + every)
        return exchange(call(functools.partial(filter_kernel, cut), ins, free(shape), scratch, flops, vmem=FILTER_VMEM)[0])

    def unpack_add(pieces, part, held):
        kernel = functools.partial(unpack_add_kernel, part * width, cut)
        scratch = [piece_buf, part_buf, table_buf, lhs, sems]
        return call(kernel, free(pieces, frames_in), free(frames_in.shape), scratch, held=held)[0]

    arrived = [pack(part) for part in range(PARTS)]
    returned = [both(pieces, part) for part, pieces in enumerate(arrived)]
    out = None
    for part, pieces in enumerate(returned):
        out = unpack_add(pieces, part, out)
    return out


def lane_taps(tap_table, first_lane, lane_count):
    channels = tap_table.shape[1]
    distinct = min(lane_count, channels)
    lane_ids = (first_lane + lax.iota(jnp.int32, distinct)) % channels
    selector = (lane_ids[None, :] == lax.iota(jnp.int32, channels)[:, None]).astype(tap_table.dtype)
    picked = jnp.dot(tap_table, selector, preferred_element_type=jnp.float32).astype(
        tap_table.dtype
    )
    return jnp.transpose(picked)


def shifted_taps(taps, base, size):
    distinct, period = taps.shape
    start = (base - (size - 1)) % period
    tiled = jnp.concatenate([taps, taps, taps], axis=1)
    window = lax.slice_in_dim(tiled, start, start + 2 * size - 1, axis=1)
    reversed_window = window[:, ::-1]
    padded = jnp.concatenate([reversed_window, jnp.zeros((distinct, 1), taps.dtype)], axis=1)
    repeated = jnp.tile(padded, (1, size + 1))
    flat = lax.slice_in_dim(repeated, size - 1, size - 1 + size * (2 * size - 1), axis=1)
    return flat.reshape(distinct, size, 2 * size - 1)[:, :, :size]


def time_convolve(segment, own_taps):
    frames, rows_here, lane_count = segment.shape
    distinct = own_taps.shape[0]
    columns = lane_count // distinct
    block_len = min(128, frames)
    block_count = frames // block_len
    blocked = segment.reshape(block_count, block_len, rows_here, columns, distinct)
    blocked = jnp.transpose(blocked, (4, 3, 2, 0, 1))
    running = jnp.zeros((distinct, columns, rows_here, block_count, block_len), jnp.float32)
    for lag_index in range(block_count):
        toeplitz = shifted_taps(own_taps, lag_index * block_len, block_len)
        rolled = jnp.roll(blocked, lag_index, axis=3)
        running = running + jnp.einsum(
            "cab,cxrnb->cxrna", toeplitz, rolled, preferred_element_type=jnp.float32
        )
    result = jnp.transpose(running, (3, 4, 2, 1, 0)).reshape(frames, rows_here, lane_count)
    return result.astype(jnp.bfloat16)


def row_convolve(segment, row_taps):
    frames, height, lane_count = segment.shape
    distinct = row_taps.shape[0]
    columns = lane_count // distinct
    arranged = jnp.transpose(segment.reshape(frames, height, columns, distinct), (3, 2, 0, 1))
    circulant = shifted_taps(row_taps, 0, height)
    filtered = jnp.einsum("cab,cxfb->cxfa", circulant, arranged, preferred_element_type=jnp.float32)
    result = jnp.transpose(filtered, (2, 3, 1, 0)).reshape(frames, height, lane_count)
    return result.astype(jnp.bfloat16)


def narrow_shards(frames_in, time_filter, height_filter):
    frames_dev, rows_dev, lane_total = frames_in.shape
    tm_count = lax.axis_size("tm")
    height_count = lax.axis_size("height")
    lane_count = lane_total // (tm_count * height_count)
    first_lane = (
        lax.axis_index("tm") * (lane_total // tm_count) + lax.axis_index("height") * lane_count
    )
    own_taps = lane_taps(time_filter, first_lane, lane_count)
    row_taps = lane_taps(height_filter, first_lane, lane_count)
    gathered = lax.all_to_all(
        lax.all_to_all(frames_in, "tm", split_axis=2, concat_axis=0, tiled=True),
        "height",
        split_axis=2,
        concat_axis=1,
        tiled=True,
    )
    temporal = time_convolve(gathered, own_taps)
    spatial_lanes = row_convolve(temporal, row_taps)
    returned = lax.all_to_all(
        lax.all_to_all(spatial_lanes, "tm", split_axis=0, concat_axis=2, tiled=True),
        "height",
        split_axis=1,
        concat_axis=2,
        tiled=True,
    )
    spatial = returned.reshape(frames_dev, rows_dev, height_count, tm_count, lane_count)
    spatial = jnp.transpose(spatial, (0, 1, 3, 2, 4)).reshape(frames_dev, rows_dev, lane_total)
    return (frames_in.astype(jnp.float32) + spatial.astype(jnp.float32)).astype(jnp.bfloat16)


def solution(mesh):
    return jax.shard_map(
        shards,
        mesh=mesh,
        in_specs=(P("tm", "height", None), P(), P()),
        out_specs=P("tm", "height", None),
        check_vma=False,
    )
```
